128 devices in a mesh: row: 4 (over y_lo, core), col: 32 (over z, x, y_hi).
Axes of the slice: x: 4, y: 4 (y_hi: 2, y_lo: 2; y = y_hi * 2 + y_lo), z: 4, core: 2. Of those that a mesh axis runs over, the one named last changes fastest.
Arguments:
- start_block: float32 [16384, 128], P(('row', 'col')), may hold values from -6 to 6
- tiles: bfloat16 [2048, 128, 128], P(('row', 'col')), may hold values from -0.1875 to 0.1875
- tile_rows: int32 [2048], P(('row', 'col')), may hold values from -1 to 31, as said below
- tile_cols: int32 [2048], P(('row', 'col')), may hold values from -1 to 3, as said below
- bounds: float32 [2], replicated, as said below
Outputs:
- basis: float32 [16384, 128], P(('row', 'col'))
The draws below stay inside these ranges and needn't reach their ends.
Inputs may be any that keep to these rules, and one draw needn't show every extreme that they name: `tile_rows`: live slots of a device come first; each device has between 4 and 16 live slots and some device has 16; empty slots hold -1. `tile_cols`: -1 exactly in the empty slots of tile_rows. bounds[0] lies in [-1.5, -0.5] and bounds[1] in [0.5, 1.5].
All inputs are finite; a program needn't handle non-finite values.
Results may differ from the reference program's by a relative error of at most 0.0003.
Values sent between devices are 32-bit elements; how exact they have to be, the bound alone decides.
No kernel may reach another device: no remote copies, remote signals or barrier semaphores. Data moves between devices by JAX's collectives and lax.ppermute only.
A program may use at most 64 MiB of HBM per device.

```python
import math
import jax
import jax.numpy as jnp
from jax import lax

BLK = 128
K = 128
BRD = 1
ITERS = 2
TD = 16
NB = 128
NV = 16384
N_ROW = 4
N_COL = 32


def slot_layout(key):
    key_col, key_one, key_two, key_live, key_pick = jax.random.split(key, 5)
    devices_all = N_ROW * N_COL
    counts = jax.random.randint(key_live, (devices_all,), 4 * BRD, TD + 1)
    chosen = jax.random.randint(key_pick, (), 0, devices_all)
    counts = counts.at[chosen].set(TD)
    slot_ids = jnp.arange(TD, dtype=jnp.int32)[None, :]
    live = slot_ids < counts[:, None]
    first_rows = jax.random.randint(key_one, (devices_all, TD), 0, BRD * N_COL)
    second_rows = jax.random.randint(key_two, (devices_all, TD), 0, BRD * N_COL)
    rows_drawn = jnp.minimum(first_rows, second_rows)
    cols_drawn = jax.random.randint(key_col, (devices_all, TD), 0, N_ROW * BRD)
    rows_drawn = jnp.where(live, rows_drawn, -1).reshape(-1).astype(jnp.int32)
    cols_drawn = jnp.where(live, cols_drawn, -1).reshape(-1).astype(jnp.int32)
    return (rows_drawn, cols_drawn)


def draw_tile_rows(key, part):
    return slot_layout(key)[0]


def draw_tile_cols(key, part):
    return slot_layout(key)[1]


def draw_bounds(key, part):
    key = jax.random.fold_in(key, 7)
    key_low, key_high = jax.random.split(key)
    lower = jax.random.uniform(key_low, (1,), jnp.float32, -1.5, -0.5)
    upper = jax.random.uniform(key_high, (1,), jnp.float32, 0.5, 1.5)
    return jnp.concatenate([lower, upper]).astype(jnp.float32)


def shard_levels(own_key, dims, shards, low, high):
    loudness = 1.0
    for dim, blocks in shards:
        heights = jax.random.uniform(jax.random.fold_in(jax.random.fold_in(own_key, 6), dim), (blocks,), jnp.float32, low / len(shards), high / len(shards))
        loudness = loudness * jnp.repeat(jnp.exp(heights), dims[dim] // blocks).reshape((-1,) + (1,) * (len(dims) - 1 - dim))
    return loudness


def noise(key, extent, width, bound, pieces=(), held_as=jnp.bfloat16):
    result = jax.random.normal(key, extent, jnp.float32) * width
    if len(pieces) > 0:
        result = shard_levels(key, extent, pieces, -0.22, 0.18) * result
    return jnp.clip(result, min=-bound, max=bound).astype(held_as)


def setup_inputs(seed: int = 0) -> dict:
    key_of = jax.random.split(jax.random.key(seed), 6)
    start_block = noise(key_of[0], (NV, K), 1.0, 6.0, ((0, 128),), jnp.float32)
    tiles = noise(key_of[1], (N_ROW * N_COL * TD, BLK, BLK), (8 * BLK) ** -0.5, 0.1875, ((0, 128),))
    tile_rows = draw_tile_rows(jax.random.fold_in(key_of[5], 71), 0)
    tile_cols = draw_tile_cols(jax.random.fold_in(key_of[5], 71), 0)
    bounds = draw_bounds(jax.random.fold_in(key_of[5], 71), 0)
    return dict(start_block=start_block, tiles=tiles, tile_rows=tile_rows, tile_cols=tile_cols, bounds=bounds)


def apply_matrix(vec_full, tiles, tile_rows, tile_cols):
    slots = jnp.arange(tiles.shape[0], dtype=jnp.int32)
    device = slots // TD
    group_row = device // N_COL
    group_col = device % N_COL
    live = tile_rows >= 0
    local_row = jnp.maximum(tile_rows, 0).astype(jnp.int32)
    local_col = jnp.maximum(tile_cols, 0).astype(jnp.int32)
    whole_row = group_row * (BRD * N_COL) + local_row
    whole_col = (local_col // BRD * N_COL + group_col) * BRD + local_col % BRD
    blocks = vec_full.reshape(NB, BLK, K)
    chosen = blocks[whole_col].astype(jnp.float32)
    prods = jnp.einsum('tij,tjk->tik', tiles.astype(jnp.float32), chosen, precision=lax.Precision.HIGHEST)
    prods = prods * live.astype(jnp.float32)[:, None, None]
    summed = jax.ops.segment_sum(prods, whole_row, NB)
    return summed.reshape(NB * BLK, K)

def reference(start_block, tiles, tile_rows, tile_cols, bounds):
    centre = (bounds[0] + bounds[1]) / 2.0
    half = (bounds[1] - bounds[0]) / 2.0

    def product(vec):
        return apply_matrix(vec, tiles, tile_rows, tile_cols)
    current = start_block
    for step in range(ITERS):
        first = (product(current) - centre * current) / half
        second = 2.0 * (product(first) - centre * first) / half - current
        third = 2.0 * (product(second) - centre * second) / half - first
        gram = jnp.dot(third.T.astype(jnp.float32), third.astype(jnp.float32), precision=lax.Precision.HIGHEST, preferred_element_type=jnp.float32)
        factor = jnp.linalg.cholesky(gram)
        current = jax.scipy.linalg.solve_triangular(factor, third.T, lower=True).T
    return current * math.sqrt(NV)
```

```python
import functools
import math

import jax
import jax.numpy as jnp
from jax import lax
from jax.experimental import pallas as pl
from jax.experimental.pallas import tpu as pltpu
from jax.sharding import Mesh
from jax.sharding import PartitionSpec as P

ITERS = 2
HIGH = lax.Precision.HIGHEST
AXES = ("ylo", "core", "zhi", "zlo", "xhi", "xlo", "yhi")
ROW = ("ylo", "core")
COL = ("zhi", "zlo", "xhi", "xlo", "yhi")
SPLIT = ("xhi", "yhi")
SCATTER = ("zhi", "zlo", "xlo")
NS = 2 ** len(SPLIT)
NM = 2 ** len(SCATTER)


def digits(index, names):
    out = 0
    for name in names:
        shift = len(COL) - 1 - COL.index(name)
        out = out * 2 + ((index >> shift) & 1)
    return out


def swap(x, name):
    return lax.ppermute(x, name, [(0, 1), (1, 0)])


def exchange(x, names):
    if not names:
        return x
    return lax.all_to_all(x, names, 0, 0, tiled=True)


def widen_kernel(t_ref, o_ref):
    o_ref[...] = t_ref[...].astype(jnp.float32)


def widen(tiles):
    return pl.pallas_call(
        widen_kernel,
        out_shape=jax.ShapeDtypeStruct(tiles.shape, jnp.float32),
        name="widen",
    )(tiles)


def pack_kernel(own_ref, *refs):
    o_ref = refs[-1]
    slots = own_ref.shape[0]
    o_ref[0:slots] = own_ref[...]
    at = slots
    for r in refs[:-1]:
        o_ref[at : at + r.shape[0]] = r[...].astype(jnp.bfloat16)
        at += r.shape[0]


def pack(own, parts):
    slots = own.shape[0] + sum(p.shape[0] for p in parts)
    return pl.pallas_call(
        pack_kernel,
        out_shape=jax.ShapeDtypeStruct((slots,) + own.shape[1:], jnp.bfloat16),
        compiler_params=pltpu.CompilerParams(vmem_limit_bytes=32 * 2**20),
        name="pack",
    )(own, *parts)


def share_tiles(tiles, rows, cols):
    half = tiles.shape[0] // 2
    meta = jnp.stack([rows, cols])
    wide = widen(tiles)
    a, b = wide[:half], wide[half:]
    a_y, b_x = swap(a, "yhi"), swap(b, "xhi")
    a_x, b_y = swap(a, "xhi"), swap(b, "yhi")
    a_xy, b_xy = swap(a_y, "xhi"), swap(b_x, "yhi")
    m_y, m_x = swap(meta, "yhi"), swap(meta, "xhi")
    m_xy = swap(m_y, "xhi")
    packed = pack(tiles, [a_y, b_y, a_x, b_x, a_xy, b_xy])
    metas = jnp.stack([meta, m_y, m_x, m_xy])
    return packed, metas[:, 0], metas[:, 1]


def product_kernel(place_ref, source_ref, v_ref, tiles_ref, o_ref, parts):
    blocks, width, blk = v_ref.shape
    v = v_ref[...]
    high = v.astype(jnp.bfloat16)
    rest = v - high.astype(jnp.float32)
    middle = rest.astype(jnp.bfloat16)
    low = (rest - middle.astype(jnp.float32)).astype(jnp.bfloat16)
    parts[0:blocks, 0:width, :] = high
    parts[0:blocks, width : 2 * width, :] = middle
    parts[0:blocks, 2 * width : 3 * width, :] = low
    parts[blocks] = jnp.zeros(parts.shape[1:], jnp.bfloat16)
    o_ref[...] = jnp.zeros_like(o_ref)

    def step(t, _):
        p = lax.dot_general(
            parts[source_ref[t]],
            tiles_ref[t],
            (((1,), (1,)), ((), ())),
            preferred_element_type=jnp.float32,
        )
        o_ref[place_ref[t]] += p[0:width] + p[width : 2 * width] + p[2 * width :]
        return 0

    lax.fori_loop(0, tiles_ref.shape[0], step, 0, unroll=UNROLL)


UNROLL = 16


def product(place, source, v, tiles, out_blocks):
    blocks, width, blk = v.shape
    smem = pl.BlockSpec(memory_space=pltpu.SMEM)
    vmem = pl.BlockSpec(memory_space=pltpu.VMEM)
    return pl.pallas_call(
        product_kernel,
        out_shape=jax.ShapeDtypeStruct((out_blocks, width, blk), jnp.float32),
        in_specs=[smem, smem, vmem, vmem],
        out_specs=vmem,
        scratch_shapes=[pltpu.VMEM((blocks + 1, 3 * width, blk), jnp.bfloat16)],
        compiler_params=pltpu.CompilerParams(vmem_limit_bytes=32 * 2**20),
        name="product",
    )(place, source, v, tiles)


def gram_sum(local):
    k = local.shape[0]
    n = 2 ** len(AXES)
    pieces = lax.all_to_all(local.reshape(n, k * k // n), AXES, 0, 0, tiled=True)
    mine = jnp.sum(pieces, axis=0)
    full = lax.all_to_all(jnp.broadcast_to(mine[None], pieces.shape), AXES, 0, 0, tiled=True)
    return full.reshape(k, k)


def on_device(start_block, tiles, tile_rows, tile_cols, bounds):
    centre = (bounds[0] + bounds[1]) / 2.0
    half = (bounds[1] - bounds[0]) / 2.0
    blk = tiles.shape[1]
    width = start_block.shape[1]
    rows = 4
    total_rows = blk * 2 ** len(AXES)
    own = 0
    for name in SPLIT:
        own = own * 2 + lax.axis_index(name)

    packed, all_rows, all_cols = share_tiles(tiles, tile_rows, tile_cols)
    live = all_rows >= 0
    position = own ^ jnp.arange(NS, dtype=jnp.int32)[:, None]
    source = jnp.where(live, all_cols * NS + position, rows * NS).reshape(-1)
    place = jnp.where(live, digits(all_rows, SCATTER) * NS + digits(all_rows, SPLIT), 0).reshape(-1)

    def apply(v):
        wide = lax.all_gather(v, ROW, axis=0, tiled=True)
        prods = product(place, source, wide, packed, NM * NS)
        got = exchange(prods.reshape(NM, NS, *v.shape[1:]), SCATTER)
        return jnp.sum(got, axis=0)

    def to_split(x):
        return exchange(x.reshape(NS, width // NS, blk), SPLIT)

    def to_whole(x):
        return exchange(x, SPLIT).reshape(width, blk)

    def filtered(current):
        first = (apply(current) - centre * current) / half
        second = 2.0 * (apply(first) - centre * first) / half - current
        return 2.0 * (apply(second) - centre * second) / half - first

    def normal_factor(x):
        local = lax.dot_general(
            x, x, (((1,), (1,)), ((), ())), precision=HIGH, preferred_element_type=jnp.float32
        )
        return jnp.linalg.cholesky(gram_sum(local))

    def solve(factor, x):
        return jax.scipy.linalg.solve_triangular(factor, x, lower=True)

    third = filtered(to_split(start_block.T))
    factor_one = normal_factor(to_whole(third))
    third = solve(factor_one, to_whole(filtered(third)))
    basis = solve(normal_factor(third), third)
    return basis.T * math.sqrt(total_rows)


def solution(mesh):
    fine = Mesh(mesh.devices.reshape((2,) * len(AXES)), AXES)
    return jax.shard_map(
        on_device,
        mesh=fine,
        in_specs=(P(AXES, None), P(AXES, None, None), P(AXES), P(AXES), P()),
        out_specs=P(AXES, None),
        check_vma=False,
    )
```

```python
import functools
import math

import jax
import jax.numpy as jnp
from jax import lax
from jax.experimental import pallas as pl
from jax.experimental.pallas import tpu as pltpu
from jax.sharding import Mesh
from jax.sharding import PartitionSpec as P

ITERS = 2
HIGH = lax.Precision.HIGHEST
AXES = ("ylo", "core", "zhi", "zlo", "xhi", "xlo", "yhi")
ROW = ("ylo", "core")
COL = ("zhi", "zlo", "xhi", "xlo", "yhi")
SPLIT = ("xhi", "yhi")
SCATTER = ("zhi", "zlo", "xlo")
NS = 2 ** len(SPLIT)
NM = 2 ** len(SCATTER)


def digits(index, names):
    out = 0
    for name in names:
        shift = len(COL) - 1 - COL.index(name)
        out = out * 2 + ((index >> shift) & 1)
    return out


def swap(x, name):
    return lax.ppermute(x, name, [(0, 1), (1, 0)])


def exchange(x, names):
    if not names:
        return x
    return lax.all_to_all(x, names, 0, 0, tiled=True)


def widen_kernel(a_ref, b_ref, wide_a_ref, wide_b_ref):
    wide_a_ref[...] = a_ref[...].astype(jnp.float32)
    wide_b_ref[...] = b_ref[...].astype(jnp.float32)


def widen(tiles):
    slots, blk, _ = tiles.shape
    step = 2
    steps = slots // 2 // step
    block = (step, blk, blk)
    first = pl.BlockSpec(block, lambda i: (i, 0, 0))
    second = pl.BlockSpec(block, lambda i: (i + steps, 0, 0))
    wide = jax.ShapeDtypeStruct((slots // 2, blk, blk), jnp.float32)
    return pl.pallas_call(
        widen_kernel,
        grid=(steps,),
        out_shape=(wide, wide),
        in_specs=[first, second],
        out_specs=(first, first),
        compiler_params=pltpu.CompilerParams(vmem_limit_bytes=48 * 2**20),
        name="widen",
    )(tiles, tiles)


def pack_kernel(*refs):
    o_ref = refs[-1]
    for i, r in enumerate(refs[:-1]):
        o_ref[i] = r[...].astype(jnp.bfloat16)


def pack(parts):
    slots, blk, _ = parts[0].shape
    step = 2
    spec = pl.BlockSpec((step, blk, blk), lambda i: (i, 0, 0))
    return pl.pallas_call(
        pack_kernel,
        grid=(slots // step,),
        out_shape=jax.ShapeDtypeStruct((len(parts), slots, blk, blk), jnp.bfloat16),
        in_specs=[spec] * len(parts),
        out_specs=pl.BlockSpec((len(parts), step, blk, blk), lambda i: (0, i, 0, 0)),
        compiler_params=pltpu.CompilerParams(vmem_limit_bytes=48 * 2**20),
        name="pack",
    )(*parts).reshape(-1, blk, blk)


def share_tiles(tiles, rows, cols):
    meta = jnp.stack([rows, cols])
    a, b = widen(tiles)
    a_y, b_x = swap(a, "yhi"), swap(b, "xhi")
    a_x, b_y = swap(a, "xhi"), swap(b, "yhi")
    a_xy, b_xy = swap(a_y, "xhi"), swap(b_x, "yhi")
    m_y, m_x = swap(meta, "yhi"), swap(meta, "xhi")
    m_xy = swap(m_y, "xhi")
    early = pack([a_y, b_y, a_x, b_x])
    late = pack([a_xy, b_xy])
    metas = jnp.stack([meta, m_y, m_x, m_xy])
    return (tiles, early, late), metas[:, 0], metas[:, 1]


def product_kernel(count, place_ref, source_ref, *refs):
    v_refs, tile_refs, o_ref, parts = refs[:count], refs[count:-2], refs[-2], refs[-1]
    blocks, width, blk = v_refs[0].shape
    for i, v_ref in enumerate(v_refs):
        v = v_ref[...]
        high = v.astype(jnp.bfloat16)
        rest = v - high.astype(jnp.float32)
        middle = rest.astype(jnp.bfloat16)
        low = (rest - middle.astype(jnp.float32)).astype(jnp.bfloat16)
        at = slice(i * blocks, (i + 1) * blocks)
        parts[at, 0:width, :] = high
        parts[at, width : 2 * width, :] = middle
        parts[at, 2 * width : 3 * width, :] = low
    parts[count * blocks] = jnp.zeros(parts.shape[1:], jnp.bfloat16)
    o_ref[...] = jnp.zeros_like(o_ref)
    base = 0
    for tiles_ref in tile_refs:
        slots = tiles_ref.shape[0]

        def step(t, _):
            p = lax.dot_general(
                parts[source_ref[base + t]],
                tiles_ref[t],
                (((1,), (1,)), ((), ())),
                preferred_element_type=jnp.float32,
            )
            o_ref[place_ref[base + t]] += p[0:width] + p[width : 2 * width] + p[2 * width :]
            return 0

        lax.fori_loop(0, slots, step, 0, unroll=16)
        base += slots


def product(place, source, vs, tiles, out_blocks):
    blocks, width, blk = vs[0].shape
    smem = pl.BlockSpec(memory_space=pltpu.SMEM)
    vmem = pl.BlockSpec(memory_space=pltpu.VMEM)
    return pl.pallas_call(
        functools.partial(product_kernel, len(vs)),
        out_shape=jax.ShapeDtypeStruct((out_blocks, width, blk), jnp.float32),
        in_specs=[smem, smem] + [vmem] * (len(vs) + len(tiles)),
        out_specs=vmem,
        scratch_shapes=[pltpu.VMEM((len(vs) * blocks + 1, 3 * width, blk), jnp.bfloat16)],
        compiler_params=pltpu.CompilerParams(vmem_limit_bytes=32 * 2**20),
        name="product",
    )(place, source, *vs, *tiles)


def factor_inverse(gram):
    size = gram.shape[0]
    count = size // 8

    def spread(x):
        return jnp.broadcast_to(x, (8, size))

    lane = lax.broadcasted_iota(jnp.int32, (8, size), 1)
    sub = lax.broadcasted_iota(jnp.int32, (8, size), 0)
    left = [gram[8 * r : 8 * r + 8, :] for r in range(count)]
    right = [jnp.where(lane == sub + 8 * r, 1.0, 0.0) for r in range(count)]
    out = []
    for p in range(count):
        steps, rows = [], []
        for r in range(p, count):
            columns = [spread(left[r][:, 8 * p + m : 8 * p + m + 1]) for m in range(8)]
            for j in range(8):
                if r == p:
                    scale = lax.rsqrt(spread(columns[j][j : j + 1, :]))
                    others = [spread(columns[m][j : j + 1, :]) * scale for m in range(j + 1, 8)]
                    steps.append((scale, others, spread(left[r][j : j + 1, :]) * scale, spread(right[r][j : j + 1, :]) * scale))
                    rows.append(steps[j][3][0:1])
                scale, others, up, row = steps[j]
                entry = columns[j] * scale
                for m in range(j + 1, 8):
                    columns[m] = columns[m] - entry * others[m - j - 1]
                left[r] = left[r] - entry * up
                right[r] = right[r] - entry * row
        out.append(jnp.concatenate(rows, axis=0))
    return out


def factor_kernel(gram_ref, o_ref):
    for i, rows in enumerate(factor_inverse(gram_ref[...])):
        o_ref[8 * i : 8 * i + 8, :] = rows


def factor(gram):
    return pl.pallas_call(factor_kernel, out_shape=jax.ShapeDtypeStruct(gram.shape, jnp.float32), name="factor")(gram)


def finish_kernel(scale, gram_ref, x_ref, o_ref, inverse):
    factor_kernel(gram_ref, inverse)
    x = jnp.dot(inverse[...], x_ref[...], precision=HIGH, preferred_element_type=jnp.float32)
    o_ref[...] = x.T * scale


def finish(gram, x, scale):
    return pl.pallas_call(
        functools.partial(finish_kernel, scale),
        out_shape=jax.ShapeDtypeStruct(x.shape[::-1], jnp.float32),
        scratch_shapes=[pltpu.VMEM(gram.shape, jnp.float32)],
        name="finish",
    )(gram, x)


def whole_blocks(refs):
    pieces = [r[i] for r in refs for i in range(r.shape[0])]
    return jnp.concatenate([jnp.concatenate(pieces[b::NS], axis=0) for b in range(NS)], axis=1)


def inner(x):
    return lax.dot_general(x, x, (((1,), (1,)), ((), ())), precision=HIGH, preferred_element_type=jnp.float32)


def gram_kernel(*refs):
    refs[-1][...] = inner(whole_blocks(refs[:-1]))


def gram(slices):
    width = slices[0].shape[1] * NS
    return pl.pallas_call(
        gram_kernel, out_shape=jax.ShapeDtypeStruct((width, width), jnp.float32), name="gram"
    )(*slices)


def normal_kernel(own_ref, inverse_ref, *refs):
    o_ref, gram_ref, all_ref = refs[-3:]
    x = whole_blocks(refs[:-3])
    y = jnp.dot(inverse_ref[...], x, precision=HIGH, preferred_element_type=jnp.float32)
    gram_ref[...] = inner(y)
    blk = o_ref.shape[1]
    for i in range(NS):
        all_ref[i] = y[:, i * blk : (i + 1) * blk]
    o_ref[...] = all_ref[own_ref[0]]


def normal(own, inverse, slices):
    width, blk = inverse.shape[0], slices[0].shape[2]
    vmem = pl.BlockSpec(memory_space=pltpu.VMEM)
    return pl.pallas_call(
        normal_kernel,
        out_shape=(
            jax.ShapeDtypeStruct((width, blk), jnp.float32),
            jax.ShapeDtypeStruct((width, width), jnp.float32),
        ),
        in_specs=[pl.BlockSpec(memory_space=pltpu.SMEM)] + [vmem] * (1 + len(slices)),
        scratch_shapes=[pltpu.VMEM((NS, width, blk), jnp.float32)],
        name="normal",
    )(own.reshape(1), inverse, *slices)


def on_device(start_block, tiles, tile_rows, tile_cols, bounds):
    centre = (bounds[0] + bounds[1]) / 2.0
    half = (bounds[1] - bounds[0]) / 2.0
    blk = tiles.shape[1]
    width = start_block.shape[1]
    total_rows = blk * 2 ** len(AXES)
    own = 0
    for name in SPLIT:
        own = own * 2 + lax.axis_index(name)
    own_row = 2 * lax.axis_index("ylo") + lax.axis_index("core")

    tile_sets, all_rows, all_cols = share_tiles(tiles, tile_rows, tile_cols)
    live = all_rows >= 0
    position = own ^ jnp.arange(NS, dtype=jnp.int32)[:, None]
    source = jnp.where(live, (all_cols ^ own_row) * NS + position, 4 * NS)
    place = jnp.where(live, digits(all_rows, SCATTER) * NS + digits(all_rows, SPLIT), 0)
    source, place = source.reshape(-1), place.reshape(-1)

    def four(v):
        return [swap(v, "core"), swap(v, "ylo"), lax.ppermute(v, ROW, [(i, i ^ 3) for i in range(4)])]

    def multiply(v, others):
        prods = product(place, source, [v, *others], tile_sets, NM * NS)
        got = exchange(prods.reshape(NM, NS, *v.shape[1:]), SCATTER)
        return jnp.sum(got, axis=0)

    def apply(v):
        return multiply(v, four(v))

    def join(x, other, name):
        low = lax.axis_index(name) == 0
        return [jnp.where(low, x, other), jnp.where(low, other, x)]

    tie = lax.optimization_barrier
    current = exchange(start_block.T.reshape(NS, width // NS, blk), SPLIT)
    first = (apply(current) - centre * current) / half
    second = 2.0 * (apply(first) - centre * first) / half - current
    third = 2.0 * (apply(second) - centre * second) / half - first

    current = third
    (others, other) = tie((four(current), swap(current, "yhi")))
    pair = jnp.concatenate(join(current, other, "yhi"), axis=0)
    first = (multiply(current, others) - centre * current) / half
    first, other = tie((first, swap(pair, "xhi")))
    others, local = tie((four(first), gram(join(pair, other, "xhi"))))
    second = 2.0 * (multiply(first, others) - centre * first) / half - current
    second, sums = tie((second, four(local)))
    local = (local + sums[0]) + (sums[1] + sums[2])
    others, other = tie((four(second), swap(local, "zlo")))
    local = local + other
    third = 2.0 * (multiply(second, others) - centre * second) / half - first
    local = local + swap(local, "zhi")
    local = local + swap(local, "xlo")
    inverse = factor(local)

    pair = jnp.concatenate(join(third, swap(third, "yhi"), "yhi"), axis=0)
    block, local = normal(own, inverse, join(pair, swap(pair, "xhi"), "xhi"))
    sums = four(local)
    local = (local + sums[0]) + (sums[1] + sums[2])
    for name in SCATTER[::-1]:
        local = local + swap(local, name)
    return finish(local, block, math.sqrt(total_rows))


def solution(mesh):
    fine = Mesh(mesh.devices.reshape((2,) * len(AXES)), AXES)
    return jax.shard_map(
        on_device,
        mesh=fine,
        in_specs=(P(AXES, None), P(AXES, None, None), P(AXES), P(AXES), P()),
        out_specs=P(AXES, None),
        check_vma=False,
    )
```

```python
import functools
import math

import jax
import jax.numpy as jnp
from jax import lax
from jax.experimental import pallas as pl
from jax.experimental.pallas import tpu as pltpu
from jax.sharding import Mesh
from jax.sharding import PartitionSpec as P

ITERS = 2
HIGH = lax.Precision.HIGHEST
AXES = ("ylo", "core", "zhi", "zlo", "xhi", "xlo", "yhi")
ROW = ("ylo", "core")
COL = ("zhi", "zlo", "xhi", "xlo", "yhi")
SPLIT = ("xhi", "yhi")
SCATTER = ("xlo", "zlo", "zhi")
NS = 2 ** len(SPLIT)
NM = 2 ** len(SCATTER)


def digits(index, names):
    out = 0
    for name in names:
        shift = len(COL) - 1 - COL.index(name)
        out = out * 2 + ((index >> shift) & 1)
    return out


def swap(x, name):
    return lax.ppermute(x, name, [(0, 1), (1, 0)])


def three(x, names):
    return [swap(x, names[1]), swap(x, names[0]), lax.ppermute(x, names, [(i, i ^ 3) for i in range(4)])]


def exchange(x, names):
    if not names:
        return x
    return lax.all_to_all(x, names, 0, 0, tiled=True)


def turn(tile):
    size = tile.shape[0]
    row = lax.broadcasted_iota(jnp.int32, (size, size), 0)
    column = lax.broadcasted_iota(jnp.int32, (size, size), 1)
    identity = jnp.where(row == column, 1.0, 0.0).astype(tile.dtype)
    return lax.dot_general(identity, tile, (((1,), (1,)), ((), ())), preferred_element_type=jnp.float32)


def widen_kernel(tiles_ref, a_ref, b_ref):
    slots, blk, _ = tiles_ref.shape
    half = slots // 2
    for i in range(half):
        a_ref[i * blk : (i + 1) * blk, :] = turn(tiles_ref[i])
        b_ref[i * blk : (i + 1) * blk, :] = turn(tiles_ref[half + i])


def widen(tiles):
    slots, blk, _ = tiles.shape
    wide = jax.ShapeDtypeStruct((slots // 2 * blk, blk), jnp.float32)
    return pl.pallas_call(
        widen_kernel,
        out_shape=(wide, wide),
        compiler_params=pltpu.CompilerParams(vmem_limit_bytes=32 * 2**20),
        name="widen",
    )(tiles)


def turn_kernel(tiles_ref, o_ref):
    for i in range(tiles_ref.shape[0]):
        o_ref[i] = turn(tiles_ref[i]).astype(o_ref.dtype)


def turn_all(tiles):
    return pl.pallas_call(
        turn_kernel, out_shape=jax.ShapeDtypeStruct(tiles.shape, tiles.dtype), name="turn"
    )(tiles)


def pack_kernel(*refs):
    o_ref = refs[-1]
    _, step, blk, _ = o_ref.shape
    for i, r in enumerate(refs[:-1]):
        for k in range(step):
            o_ref[i, k] = r[k * blk : (k + 1) * blk, :].astype(o_ref.dtype)


def pack(parts, slots):
    blk = parts[0].shape[1]
    step = 4
    spec = pl.BlockSpec((step * blk, blk), lambda i: (i, 0))
    return pl.pallas_call(
        pack_kernel,
        grid=(slots // step,),
        out_shape=jax.ShapeDtypeStruct((len(parts), slots, blk, blk), jnp.bfloat16),
        in_specs=[spec] * len(parts),
        out_specs=pl.BlockSpec((len(parts), step, blk, blk), lambda i: (0, i, 0, 0)),
        compiler_params=pltpu.CompilerParams(vmem_limit_bytes=32 * 2**20),
        name="pack",
    )(*parts).reshape(-1, blk, blk)


def share_tiles(tiles, small):
    half = tiles.shape[0] // 2
    a, b = widen(tiles)
    a_y, b_x = swap(a, "yhi"), swap(b, "xhi")
    a_x, b_y = swap(a, "xhi"), swap(b, "yhi")
    a_y, b_x, small = lax.optimization_barrier((a_y, b_x, small))
    a_xy, b_xy = swap(a_y, "xhi"), swap(b_x, "yhi")
    _, tiles = lax.optimization_barrier((a_x, tiles))
    return (turn_all(tiles), pack([a_y, b_y, a_x, b_x], half), pack([a_xy, b_xy], half)), small


def product_kernel(count, begun, start, own_ref, place_ref, source_ref, *refs):
    v_refs, tile_refs, o_ref, parts = refs[:count], refs[count : -2 - begun], refs[-2], refs[-1]
    blocks, width, blk = v_refs[0].shape
    for i, v_ref in enumerate(v_refs):
        v = v_ref[...]
        high = v.astype(jnp.bfloat16)
        rest = v - high.astype(jnp.float32)
        middle = rest.astype(jnp.bfloat16)
        low = (rest - middle.astype(jnp.float32)).astype(jnp.bfloat16)
        at = slice(i * blocks, (i + 1) * blocks)
        parts[at, 0:width, :] = high
        parts[at, width : 2 * width, :] = middle
        parts[at, 2 * width : 3 * width, :] = low
    parts[count * blocks] = jnp.zeros(parts.shape[1:], jnp.bfloat16)
    o_ref[...] = refs[-3][...] if begun else jnp.zeros_like(o_ref)
    slots = place_ref.shape[0] // NS
    at = start
    for tiles_ref in tile_refs:
        for t in range(tiles_ref.shape[0]):
            slot = (own_ref[0] ^ (at // slots)) * slots + at % slots
            at += 1
            p = lax.dot_general(
                parts[source_ref[slot]],
                tiles_ref[t],
                (((1,), (0,)), ((), ())),
                preferred_element_type=jnp.float32,
            )
            o_ref[place_ref[slot]] += p[0:width] + p[width : 2 * width] + p[2 * width :]


def product(own, place, source, vs, tiles, out_blocks, start=0, begun=None):
    blocks, width, blk = vs[0].shape
    smem = pl.BlockSpec(memory_space=pltpu.SMEM)
    vmem = pl.BlockSpec(memory_space=pltpu.VMEM)
    return pl.pallas_call(
        functools.partial(product_kernel, len(vs), begun is not None, start),
        out_shape=jax.ShapeDtypeStruct((out_blocks, width, blk), jnp.float32),
        in_specs=[smem] * 3 + [vmem] * (len(vs) + len(tiles) + (begun is not None)),
        out_specs=vmem,
        scratch_shapes=[pltpu.VMEM((len(vs) * blocks + 1, 3 * width, blk), jnp.bfloat16)],
        compiler_params=pltpu.CompilerParams(vmem_limit_bytes=32 * 2**20),
        name="product",
    )(own.reshape(1), place, source, *vs, *tiles, *([] if begun is None else [begun]))


def factor_solve(gram, right):
    size = gram.shape[0]
    count = size // 8

    def spread(x):
        return jnp.broadcast_to(x, (8, size))

    left = [gram[8 * r : 8 * r + 8, :] for r in range(count)]
    right = list(right)
    out = []
    for p in range(count):
        steps, rows = [], []
        for r in range(p, count):
            columns = [spread(left[r][:, 8 * p + m : 8 * p + m + 1]) for m in range(8)]
            for j in range(8):
                if r == p:
                    scale = lax.rsqrt(spread(columns[j][j : j + 1, :]))
                    others = [spread(columns[m][j : j + 1, :]) * scale for m in range(j + 1, 8)]
                    steps.append((scale, others, spread(left[r][j : j + 1, :]) * scale, spread(right[r][j : j + 1, :]) * scale))
                    rows.append(steps[j][3][0:1])
                scale, others, up, row = steps[j]
                entry = columns[j] * scale
                for m in range(j + 1, 8):
                    columns[m] = columns[m] - entry * others[m - j - 1]
                left[r] = left[r] - entry * up
                right[r] = right[r] - entry * row
        out.append(jnp.concatenate(rows, axis=0))
    return out


def factor_kernel(gram_ref, o_ref):
    size = gram_ref.shape[0]
    lane = lax.broadcasted_iota(jnp.int32, (8, size), 1)
    sub = lax.broadcasted_iota(jnp.int32, (8, size), 0)
    identity = [jnp.where(lane == sub + 8 * r, 1.0, 0.0) for r in range(size // 8)]
    for i, rows in enumerate(factor_solve(gram_ref[...], identity)):
        o_ref[8 * i : 8 * i + 8, :] = rows


def factor(gram):
    return pl.pallas_call(factor_kernel, out_shape=jax.ShapeDtypeStruct(gram.shape, jnp.float32), name="factor")(gram)


def finish_kernel(scale, gram_ref, other_ref, x_ref, o_ref):
    x = [x_ref[8 * r : 8 * r + 8, :] for r in range(x_ref.shape[0] // 8)]
    x = factor_solve(gram_ref[...] + other_ref[...], x)
    o_ref[...] = jnp.concatenate(x, axis=0).T * scale


def finish(gram, other, x, scale):
    return pl.pallas_call(
        functools.partial(finish_kernel, scale),
        out_shape=jax.ShapeDtypeStruct(x.shape[::-1], jnp.float32),
        compiler_params=pltpu.CompilerParams(vmem_limit_bytes=56 * 2**20),
        name="finish",
    )(gram, other, x)


def join(own, refs, x_ref):
    for i, r in enumerate(refs):
        blocks, width, blk = r.shape
        rows = pl.ds(pl.multiple_of((own ^ i) * width, width), width)
        for b in range(blocks):
            x_ref[rows, b * blk : (b + 1) * blk] = r[b]


def inner(x):
    return lax.dot_general(x, x, (((1,), (1,)), ((), ())), precision=HIGH, preferred_element_type=jnp.float32)


def gram_kernel(own_ref, *refs):
    o_ref, x_ref = refs[-2:]
    join(own_ref[0], refs[:-2], x_ref)
    o_ref[...] = inner(x_ref[...])


def gram(own, slices):
    blocks, width, blk = slices[0].shape
    width *= len(slices)
    vmem = pl.BlockSpec(memory_space=pltpu.VMEM)
    return pl.pallas_call(
        gram_kernel,
        out_shape=jax.ShapeDtypeStruct((width, width), jnp.float32),
        in_specs=[pl.BlockSpec(memory_space=pltpu.SMEM)] + [vmem] * len(slices),
        scratch_shapes=[pltpu.VMEM((width, blocks * blk), jnp.float32)],
        name="gram",
    )(own.reshape(1), *slices)


def normal_kernel(own_ref, inverse_ref, *refs):
    o_ref, gram_ref, x_ref, all_ref = refs[-4:]
    join(own_ref[0], refs[:-4], x_ref)
    y = jnp.dot(inverse_ref[...], x_ref[...], precision=HIGH, preferred_element_type=jnp.float32)
    gram_ref[...] = inner(y)
    blk = o_ref.shape[1]
    for i in range(all_ref.shape[0]):
        all_ref[i] = y[:, i * blk : (i + 1) * blk]
    o_ref[...] = all_ref[own_ref[0]]


def normal(own, inverse, slices):
    blocks, width, blk = slices[0].shape
    width *= len(slices)
    vmem = pl.BlockSpec(memory_space=pltpu.VMEM)
    return pl.pallas_call(
        normal_kernel,
        out_shape=(
            jax.ShapeDtypeStruct((width, blk), jnp.float32),
            jax.ShapeDtypeStruct((width, width), jnp.float32),
        ),
        in_specs=[pl.BlockSpec(memory_space=pltpu.SMEM)] + [vmem] * (1 + len(slices)),
        scratch_shapes=[
            pltpu.VMEM((width, blocks * blk), jnp.float32),
            pltpu.VMEM((blocks, width, blk), jnp.float32),
        ],
        compiler_params=pltpu.CompilerParams(vmem_limit_bytes=56 * 2**20),
        name="normal",
    )(own.reshape(1), inverse, *slices)


def ends_kernel(bounds_ref, centre_ref, half_ref):
    centre_ref[...] = jnp.full(centre_ref.shape, (bounds_ref[0] + bounds_ref[1]) / 2.0)
    half_ref[...] = jnp.full(half_ref.shape, (bounds_ref[1] - bounds_ref[0]) / 2.0)


def ends(bounds, width):
    row = jax.ShapeDtypeStruct((1, width), jnp.float32)
    return pl.pallas_call(
        ends_kernel, out_shape=(row, row), in_specs=[pl.BlockSpec(memory_space=pltpu.SMEM)], name="ends"
    )(bounds)


def on_device(start_block, tiles, tile_rows, tile_cols, bounds):
    blk = tiles.shape[1]
    centre, half = ends(bounds, blk)
    width = start_block.shape[1]
    total_rows = blk * 2 ** len(AXES)
    own = 0
    for name in SPLIT:
        own = own * 2 + lax.axis_index(name)
    own_row = 2 * lax.axis_index("ylo") + lax.axis_index("core")
    tie = lax.optimization_barrier

    start_block, centre, half = tie((start_block, centre, half))
    slots = tile_rows.shape[0]
    notes = jnp.pad(jnp.stack([tile_rows, tile_cols]).astype(jnp.float32), ((0, 6), (0, blk - slots)))
    slices = start_block.T.reshape(NS, width // NS, blk)
    slices = jnp.concatenate([slices, jnp.broadcast_to(notes, (NS, *notes.shape))], axis=1)
    got = exchange(jnp.broadcast_to(slices, (4, *slices.shape)).reshape(4 * NS, *slices.shape[1:]), ROW + SPLIT)
    tile_sets, got = share_tiles(tiles, got)
    begun = got[:, : width // NS]
    got = lax.dynamic_index_in_dim(got.reshape(4, NS, *got.shape[1:]), own_row, 0, keepdims=False)
    current = got[:, : width // NS]
    all_rows, all_cols = (got[:, width // NS + i, :slots].astype(jnp.int32) for i in range(2))
    live = all_rows >= 0
    member = jnp.arange(NS, dtype=jnp.int32)[:, None]
    source = jnp.where(live, (all_cols ^ own_row) * NS + member, 4 * NS).reshape(-1)
    source_begun = jnp.where(live, all_cols * NS + member, 4 * NS).reshape(-1)
    place = jnp.where(live, digits(all_rows, SCATTER) * NS + digits(all_rows, SPLIT), 0).reshape(-1)
    early = sum(t.shape[0] for t in tile_sets[:-1])

    def add_up(prods):
        return jnp.sum(exchange(prods.reshape(NM, NS, width // NS, blk), SCATTER), axis=0)

    def multiply(v, others):
        return add_up(product(own, place, source, [v, *others], tile_sets, NM * NS))

    def multiply_first(v):
        prods = product(own, place, source_begun, [v], tile_sets[:-1], NM * NS)
        return add_up(product(own, place, source_begun, [v], tile_sets[-1:], NM * NS, early, prods))

    def apply(v):
        return multiply(v, three(v, ROW))

    def add_three(x, others):
        return (x + others[0]) + (others[1] + others[2])

    first = (multiply_first(begun) - centre * current) / half
    second = 2.0 * (apply(first) - centre * first) / half - current
    third = 2.0 * (apply(second) - centre * second) / half - first

    current = third
    first = (apply(current) - centre * current) / half
    first, slices = tie((first, three(current, SPLIT)))
    others, local = tie((three(first, ROW), gram(own, [current, *slices])))
    second = 2.0 * (multiply(first, others) - centre * first) / half - current
    second, sums = tie((second, three(local, ROW)))
    local = add_three(local, sums)
    others, other = tie((three(second, ROW), swap(local, "zhi")))
    local = local + other
    third = 2.0 * (multiply(second, others) - centre * second) / half - first
    third, sums = tie((third, three(local, ("zlo", "xlo"))))
    inverse = factor(add_three(local, sums))

    block, local = normal(own, inverse, [third, *three(third, SPLIT)])
    local = add_three(local, three(local, ROW))
    local = add_three(local, three(local, ("zlo", "xlo")))
    return finish(local, swap(local, "zhi"), block, math.sqrt(total_rows))


def solution(mesh):
    fine = Mesh(mesh.devices.reshape((2,) * len(AXES)), AXES)
    return jax.shard_map(
        on_device,
        mesh=fine,
        in_specs=(P(AXES, None), P(AXES, None, None), P(AXES), P(AXES), P()),
        out_specs=P(AXES, None),
        check_vma=False,
    )
```

```python
import functools
import math

import jax
import jax.numpy as jnp
from jax import lax
from jax.experimental import pallas as pl
from jax.experimental.pallas import tpu as pltpu
from jax.sharding import Mesh
from jax.sharding import PartitionSpec as P

ITERS = 2
HIGH = lax.Precision.HIGHEST
AXES = ("ylo", "core", "zhi", "zlo", "xhi", "xlo", "yhi")
ROW = ("ylo", "core")
COL = ("zhi", "zlo", "xhi", "xlo", "yhi")
SPLIT = ("xhi", "yhi")
SCATTER = ("xlo", "zlo", "zhi")
NS = 2 ** len(SPLIT)
NM = 2 ** len(SCATTER)


def digits(index, names):
    out = 0
    for name in names:
        shift = len(COL) - 1 - COL.index(name)
        out = out * 2 + ((index >> shift) & 1)
    return out


def swap(x, name):
    return lax.ppermute(x, name, [(0, 1), (1, 0)])


def three(x, names):
    return [swap(x, names[1]), swap(x, names[0]), lax.ppermute(x, names, [(i, i ^ 3) for i in range(4)])]


def exchange(x, names):
    if not names:
        return x
    return lax.all_to_all(x, names, 0, 0, tiled=True)


def turn(tile):
    size = tile.shape[0]
    row = lax.broadcasted_iota(jnp.int32, (size, size), 0)
    column = lax.broadcasted_iota(jnp.int32, (size, size), 1)
    identity = jnp.where(row == column, 1.0, 0.0).astype(tile.dtype)
    return lax.dot_general(identity, tile, (((1,), (1,)), ((), ())), preferred_element_type=jnp.float32)


def widen_kernel(tiles_ref, a_ref, b_ref):
    slots, blk, _ = tiles_ref.shape
    half = slots // 2
    for i in range(half):
        a_ref[i * blk : (i + 1) * blk, :] = turn(tiles_ref[i])
        b_ref[i * blk : (i + 1) * blk, :] = turn(tiles_ref[half + i])


def widen(tiles):
    slots, blk, _ = tiles.shape
    wide = jax.ShapeDtypeStruct((slots // 2 * blk, blk), jnp.float32)
    return pl.pallas_call(
        widen_kernel,
        out_shape=(wide, wide),
        compiler_params=pltpu.CompilerParams(vmem_limit_bytes=32 * 2**20),
        name="widen",
    )(tiles)


def turn_kernel(tiles_ref, o_ref):
    for i in range(tiles_ref.shape[0]):
        o_ref[i] = turn(tiles_ref[i]).astype(o_ref.dtype)


def turn_all(tiles):
    return pl.pallas_call(
        turn_kernel, out_shape=jax.ShapeDtypeStruct(tiles.shape, tiles.dtype), name="turn"
    )(tiles)


def pack_kernel(*refs):
    o_ref = refs[-1]
    _, step, blk, _ = o_ref.shape
    for i, r in enumerate(refs[:-1]):
        for k in range(step):
            o_ref[i, k] = r[k * blk : (k + 1) * blk, :].astype(o_ref.dtype)


def pack(parts, slots):
    blk = parts[0].shape[1]
    step = 4
    spec = pl.BlockSpec((step * blk, blk), lambda i: (i, 0))
    return pl.pallas_call(
        pack_kernel,
        grid=(slots // step,),
        out_shape=jax.ShapeDtypeStruct((len(parts), slots, blk, blk), jnp.bfloat16),
        in_specs=[spec] * len(parts),
        out_specs=pl.BlockSpec((len(parts), step, blk, blk), lambda i: (0, i, 0, 0)),
        compiler_params=pltpu.CompilerParams(vmem_limit_bytes=32 * 2**20),
        name="pack",
    )(*parts).reshape(-1, blk, blk)


def share_tiles(tiles, small):
    half = tiles.shape[0] // 2
    a, b = widen(tiles)
    a_y, b_x = swap(a, "yhi"), swap(b, "xhi")
    a_x, b_y = swap(a, "xhi"), swap(b, "yhi")
    a_xy, b_xy = swap(a_y, "xhi"), swap(b_x, "yhi")
    _, tiles = lax.optimization_barrier((a_x, tiles))
    return (turn_all(tiles), pack([a_y, b_y, a_x, b_x], half), pack([a_xy, b_xy], half)), small


def product_kernel(count, begun, start, own_ref, place_ref, source_ref, *refs):
    v_refs, tile_refs, o_ref, parts = refs[:count], refs[count : -2 - begun], refs[-2], refs[-1]
    blocks, width, blk = v_refs[0].shape
    for i, v_ref in enumerate(v_refs):
        v = v_ref[...]
        high = v.astype(jnp.bfloat16)
        rest = v - high.astype(jnp.float32)
        middle = rest.astype(jnp.bfloat16)
        low = (rest - middle.astype(jnp.float32)).astype(jnp.bfloat16)
        at = slice(i * blocks, (i + 1) * blocks)
        parts[at, 0:width, :] = high
        parts[at, width : 2 * width, :] = middle
        parts[at, 2 * width : 3 * width, :] = low
    parts[count * blocks] = jnp.zeros(parts.shape[1:], jnp.bfloat16)
    o_ref[...] = refs[-3][...] if begun else jnp.zeros_like(o_ref)
    slots = place_ref.shape[0] // NS
    at = start
    for tiles_ref in tile_refs:
        for t in range(tiles_ref.shape[0]):
            slot = (own_ref[0] ^ (at // slots)) * slots + at % slots
            at += 1
            p = lax.dot_general(
                parts[source_ref[slot]],
                tiles_ref[t],
                (((1,), (0,)), ((), ())),
                preferred_element_type=jnp.float32,
            )
            o_ref[place_ref[slot]] += p[0:width] + p[width : 2 * width] + p[2 * width :]


def product(own, place, source, vs, tiles, out_blocks, start=0, begun=None):
    blocks, width, blk = vs[0].shape
    smem = pl.BlockSpec(memory_space=pltpu.SMEM)
    vmem = pl.BlockSpec(memory_space=pltpu.VMEM)
    return pl.pallas_call(
        functools.partial(product_kernel, len(vs), begun is not None, start),
        out_shape=jax.ShapeDtypeStruct((out_blocks, width, blk), jnp.float32),
        in_specs=[smem] * 3 + [vmem] * (len(vs) + len(tiles) + (begun is not None)),
        out_specs=vmem,
        scratch_shapes=[pltpu.VMEM((len(vs) * blocks + 1, 3 * width, blk), jnp.bfloat16)],
        compiler_params=pltpu.CompilerParams(vmem_limit_bytes=32 * 2**20),
        name="product",
    )(own.reshape(1), place, source, *vs, *tiles, *([] if begun is None else [begun]))


def factor_solve(gram, right):
    size = gram.shape[0]
    count = size // 8

    def spread(x):
        return jnp.broadcast_to(x, (8, size))

    left = [gram[8 * r : 8 * r + 8, :] for r in range(count)]
    right = list(right)
    out = []
    for p in range(count):
        steps, rows = [], []
        for r in range(p, count):
            columns = [spread(left[r][:, 8 * p + m : 8 * p + m + 1]) for m in range(8)]
            for j in range(8):
                if r == p:
                    scale = lax.rsqrt(spread(columns[j][j : j + 1, :]))
                    others = [spread(columns[m][j : j + 1, :]) * scale for m in range(j + 1, 8)]
                    steps.append((scale, others, spread(left[r][j : j + 1, :]) * scale, spread(right[r][j : j + 1, :]) * scale))
                    rows.append(steps[j][3][0:1])
                scale, others, up, row = steps[j]
                entry = columns[j] * scale
                for m in range(j + 1, 8):
                    columns[m] = columns[m] - entry * others[m - j - 1]
                left[r] = left[r] - entry * up
                right[r] = right[r] - entry * row
        out.append(jnp.concatenate(rows, axis=0))
    return out


def factor_kernel(gram_ref, o_ref):
    size = gram_ref.shape[0]
    lane = lax.broadcasted_iota(jnp.int32, (8, size), 1)
    sub = lax.broadcasted_iota(jnp.int32, (8, size), 0)
    identity = [jnp.where(lane == sub + 8 * r, 1.0, 0.0) for r in range(size // 8)]
    for i, rows in enumerate(factor_solve(gram_ref[...], identity)):
        o_ref[8 * i : 8 * i + 8, :] = rows


def factor(gram):
    return pl.pallas_call(factor_kernel, out_shape=jax.ShapeDtypeStruct(gram.shape, jnp.float32), name="factor")(gram)


def fold(gram):
    half = gram.shape[0] // 2
    row = lax.broadcasted_iota(jnp.int32, (half, 2 * half), 0)
    column = lax.broadcasted_iota(jnp.int32, (half, 2 * half), 1) - half
    top, low = gram[:half], gram[half:]
    body = jnp.where((column < 0) | (row < column), low, pltpu.roll(top, half, 1))
    diagonal = jnp.sum(jnp.where(row == column, low, 0.0), axis=0, keepdims=True)
    return jnp.concatenate([body, jnp.broadcast_to(diagonal, (8, 2 * half))], axis=0)


def unfold(folded):
    half = folded.shape[1] // 2
    row = lax.broadcasted_iota(jnp.int32, (half, 2 * half), 0)
    column = lax.broadcasted_iota(jnp.int32, (half, 2 * half), 1)
    body, diagonal = folded[:half], folded[half : half + 1]
    turned = jnp.concatenate([body, jnp.zeros_like(body)], axis=0).T
    beside, below = turned[:half], turned[half:]
    first = jnp.where(row >= column, pltpu.roll(body, half, 1), below)
    top = jnp.where(column < half, first, pltpu.roll(beside, half, 1))
    column = column - half
    last = jnp.where(row == column, diagonal, pltpu.roll(below, half, 1))
    low = jnp.where((column < 0) | (row < column), body, last)
    return jnp.concatenate([top, low], axis=0)


def finish_kernel(scale, folded_ref, x_ref, o_ref):
    folded = folded_ref[0]
    for i in range(1, folded_ref.shape[0]):
        folded = folded + folded_ref[i]
    x = [x_ref[8 * r : 8 * r + 8, :] for r in range(x_ref.shape[0] // 8)]
    x = factor_solve(unfold(folded), x)
    o_ref[...] = jnp.concatenate(x, axis=0).T * scale


def finish(folded, x, scale):
    return pl.pallas_call(
        functools.partial(finish_kernel, scale),
        out_shape=jax.ShapeDtypeStruct(x.shape[::-1], jnp.float32),
        compiler_params=pltpu.CompilerParams(vmem_limit_bytes=32 * 2**20),
        name="finish",
    )(folded, x)


def join(own, refs, x_ref):
    for i, r in enumerate(refs):
        blocks, width, blk = r.shape
        rows = pl.ds(pl.multiple_of((own ^ i) * width, width), width)
        for b in range(blocks):
            x_ref[rows, b * blk : (b + 1) * blk] = r[b]


def inner(x):
    return lax.dot_general(x, x, (((1,), (1,)), ((), ())), precision=HIGH, preferred_element_type=jnp.float32)


def gram_kernel(own_ref, *refs):
    o_ref, x_ref = refs[-2:]
    join(own_ref[0], refs[:-2], x_ref)
    o_ref[...] = inner(x_ref[...])


def gram(own, slices):
    blocks, width, blk = slices[0].shape
    width *= len(slices)
    vmem = pl.BlockSpec(memory_space=pltpu.VMEM)
    return pl.pallas_call(
        gram_kernel,
        out_shape=jax.ShapeDtypeStruct((width, width), jnp.float32),
        in_specs=[pl.BlockSpec(memory_space=pltpu.SMEM)] + [vmem] * len(slices),
        scratch_shapes=[pltpu.VMEM((width, blocks * blk), jnp.float32)],
        name="gram",
    )(own.reshape(1), *slices)


def normal_kernel(own_ref, inverse_ref, *refs):
    o_ref, gram_ref, x_ref, all_ref = refs[-4:]
    join(own_ref[0], refs[:-4], x_ref)
    y = jnp.dot(inverse_ref[...], x_ref[...], precision=HIGH, preferred_element_type=jnp.float32)
    gram_ref[...] = fold(inner(y))
    blk = o_ref.shape[1]
    for i in range(all_ref.shape[0]):
        all_ref[i] = y[:, i * blk : (i + 1) * blk]
    o_ref[...] = all_ref[own_ref[0]]


def normal(own, inverse, slices):
    blocks, width, blk = slices[0].shape
    width *= len(slices)
    vmem = pl.BlockSpec(memory_space=pltpu.VMEM)
    return pl.pallas_call(
        normal_kernel,
        out_shape=(
            jax.ShapeDtypeStruct((width, blk), jnp.float32),
            jax.ShapeDtypeStruct((width // 2 + 8, width), jnp.float32),
        ),
        in_specs=[pl.BlockSpec(memory_space=pltpu.SMEM)] + [vmem] * (1 + len(slices)),
        scratch_shapes=[
            pltpu.VMEM((width, blocks * blk), jnp.float32),
            pltpu.VMEM((blocks, width, blk), jnp.float32),
        ],
        compiler_params=pltpu.CompilerParams(vmem_limit_bytes=56 * 2**20),
        name="normal",
    )(own.reshape(1), inverse, *slices)


def ends_kernel(bounds_ref, centre_ref, half_ref):
    centre_ref[...] = jnp.full(centre_ref.shape, (bounds_ref[0] + bounds_ref[1]) / 2.0)
    half_ref[...] = jnp.full(half_ref.shape, (bounds_ref[1] - bounds_ref[0]) / 2.0)


def ends(bounds, width):
    row = jax.ShapeDtypeStruct((1, width), jnp.float32)
    return pl.pallas_call(
        ends_kernel, out_shape=(row, row), in_specs=[pl.BlockSpec(memory_space=pltpu.SMEM)], name="ends"
    )(bounds)


def on_device(start_block, tiles, tile_rows, tile_cols, bounds):
    blk = tiles.shape[1]
    centre, half = ends(bounds, blk)
    width = start_block.shape[1]
    total_rows = blk * 2 ** len(AXES)
    own = 0
    for name in SPLIT:
        own = own * 2 + lax.axis_index(name)
    own_row = 2 * lax.axis_index("ylo") + lax.axis_index("core")
    tie = lax.optimization_barrier

    start_block, centre, half = tie((start_block, centre, half))
    slots = tile_rows.shape[0]
    notes = jnp.pad(jnp.stack([tile_rows, tile_cols]).astype(jnp.float32), ((0, 6), (0, blk - slots)))
    slices = start_block.T.reshape(NS, width // NS, blk)
    slices = jnp.concatenate([slices, jnp.broadcast_to(notes, (NS, *notes.shape))], axis=1)
    got = exchange(jnp.broadcast_to(slices, (4, *slices.shape)).reshape(4 * NS, *slices.shape[1:]), ROW + SPLIT)
    tile_sets, got = share_tiles(tiles, got)
    begun = got[:, : width // NS]
    got = lax.dynamic_index_in_dim(got.reshape(4, NS, *got.shape[1:]), own_row, 0, keepdims=False)
    current = got[:, : width // NS]
    all_rows, all_cols = (got[:, width // NS + i, :slots].astype(jnp.int32) for i in range(2))
    live = all_rows >= 0
    member = jnp.arange(NS, dtype=jnp.int32)[:, None]
    source = jnp.where(live, (all_cols ^ own_row) * NS + member, 4 * NS).reshape(-1)
    source_begun = jnp.where(live, all_cols * NS + member, 4 * NS).reshape(-1)
    place = jnp.where(live, digits(all_rows, SCATTER) * NS + digits(all_rows, SPLIT), 0).reshape(-1)
    early = sum(t.shape[0] for t in tile_sets[:-1])

    def add_up(prods):
        return jnp.sum(exchange(prods.reshape(NM, NS, width // NS, blk), SCATTER), axis=0)

    def multiply(v, others):
        return add_up(product(own, place, source, [v, *others], tile_sets, NM * NS))

    def multiply_first(v):
        prods = product(own, place, source_begun, [v], tile_sets[:-1], NM * NS)
        return add_up(product(own, place, source_begun, [v], tile_sets[-1:], NM * NS, early, prods))

    def apply(v):
        return multiply(v, three(v, ROW))

    def add_three(x, others):
        return (x + others[0]) + (others[1] + others[2])

    first = (multiply_first(begun) - centre * current) / half
    second = 2.0 * (apply(first) - centre * first) / half - current
    third = 2.0 * (apply(second) - centre * second) / half - first

    current = third
    first = (apply(current) - centre * current) / half
    slices = three(current, SPLIT)
    first, *slices[:2] = tie((first, *slices[:2]))
    others, slices[2] = tie((three(first, ROW), slices[2]))
    second = 2.0 * (multiply(first, others) - centre * first) / half - current
    local = gram(own, [current, *slices])
    second, sums = tie((second, three(local, ROW)))
    local = add_three(local, sums)
    others, other = tie((three(second, ROW), swap(local, "zhi")))
    local = local + other
    third = 2.0 * (multiply(second, others) - centre * second) / half - first
    third, sums = tie((third, three(local, ("zlo", "xlo"))))
    inverse = factor(add_three(local, sums))

    block, local = normal(own, inverse, [third, *three(third, SPLIT)])
    local = add_three(local, three(local, ROW))
    folded = exchange(jnp.broadcast_to(local, (NM, *local.shape)), SCATTER)
    return finish(folded, block, math.sqrt(total_rows))


def solution(mesh):
    fine = Mesh(mesh.devices.reshape((2,) * len(AXES)), AXES)
    return jax.shard_map(
        on_device,
        mesh=fine,
        in_specs=(P(AXES, None), P(AXES, None, None), P(AXES), P(AXES), P()),
        out_specs=P(AXES, None),
        check_vma=False,
    )
```

```python
import functools
import math

import jax
import jax.numpy as jnp
from jax import lax
from jax.experimental import pallas as pl
from jax.experimental.pallas import tpu as pltpu
from jax.sharding import Mesh
from jax.sharding import PartitionSpec as P

ITERS = 2
HIGH = lax.Precision.HIGHEST
AXES = ("ylo", "core", "zhi", "zlo", "xhi", "xlo", "yhi")
ROW = ("ylo", "core")
COL = ("zhi", "zlo", "xhi", "xlo", "yhi")
SPLIT = ("xhi", "yhi")
SCATTER = ("xlo", "zlo", "zhi")
NS = 2 ** len(SPLIT)
NM = 2 ** len(SCATTER)
GRANT = pltpu.CompilerParams(vmem_limit_bytes=16 * 2**20)


def digits(index, names):
    out = 0
    for name in names:
        shift = len(COL) - 1 - COL.index(name)
        out = out * 2 + ((index >> shift) & 1)
    return out


def swap(x, name):
    return lax.ppermute(x, name, [(0, 1), (1, 0)])


def three(x, names):
    return [swap(x, names[1]), swap(x, names[0]), lax.ppermute(x, names, [(i, i ^ 3) for i in range(4)])]


def exchange(x, names):
    if not names:
        return x
    return lax.all_to_all(x, names, 0, 0, tiled=True)


def turn(tile):
    size = tile.shape[0]
    row = lax.broadcasted_iota(jnp.int32, (size, size), 0)
    column = lax.broadcasted_iota(jnp.int32, (size, size), 1)
    identity = jnp.where(row == column, 1.0, 0.0).astype(tile.dtype)
    return lax.dot_general(identity, tile, (((1,), (1,)), ((), ())), preferred_element_type=jnp.float32)


def widen_kernel(tiles_ref, a_ref, b_ref):
    slots, blk, _ = tiles_ref.shape
    half = slots // 2
    for i in range(half):
        a_ref[i * blk : (i + 1) * blk, :] = turn(tiles_ref[i])
        b_ref[i * blk : (i + 1) * blk, :] = turn(tiles_ref[half + i])


def widen(tiles):
    slots, blk, _ = tiles.shape
    wide = jax.ShapeDtypeStruct((slots // 2 * blk, blk), jnp.float32)
    return pl.pallas_call(
        widen_kernel,
        out_shape=(wide, wide),
        compiler_params=GRANT,
        name="widen",
    )(tiles)


def turn_kernel(tiles_ref, o_ref):
    for i in range(tiles_ref.shape[0]):
        o_ref[i] = turn(tiles_ref[i]).astype(o_ref.dtype)


def turn_all(tiles):
    return pl.pallas_call(
        turn_kernel,
        out_shape=jax.ShapeDtypeStruct(tiles.shape, tiles.dtype),
        compiler_params=GRANT,
        name="turn",
    )(tiles)


def pack_kernel(*refs):
    o_ref = refs[-1]
    _, step, blk, _ = o_ref.shape
    for i, r in enumerate(refs[:-1]):
        for k in range(step):
            o_ref[i, k] = r[k * blk : (k + 1) * blk, :].astype(o_ref.dtype)


def pack(parts, slots):
    blk = parts[0].shape[1]
    step = 4
    spec = pl.BlockSpec((step * blk, blk), lambda i: (i, 0))
    return pl.pallas_call(
        pack_kernel,
        grid=(slots // step,),
        out_shape=jax.ShapeDtypeStruct((len(parts), slots, blk, blk), jnp.bfloat16),
        in_specs=[spec] * len(parts),
        out_specs=pl.BlockSpec((len(parts), step, blk, blk), lambda i: (0, i, 0, 0)),
        compiler_params=GRANT,
        name="pack",
    )(*parts).reshape(-1, blk, blk)


def share_tiles(tiles, small):
    half = tiles.shape[0] // 2
    a, b = widen(tiles)
    a_y, b_x = swap(a, "yhi"), swap(b, "xhi")
    a_x, b_y = swap(a, "xhi"), swap(b, "yhi")
    a_xy, b_xy = swap(a_y, "xhi"), swap(b_x, "yhi")
    _, tiles = lax.optimization_barrier((a_x, tiles))
    return (turn_all(tiles), pack([a_y, b_y, a_x, b_x], half), pack([a_xy, b_xy], half)), small


def product_kernel(count, begun, rider, start, own_ref, place_ref, source_ref, *refs):
    v_refs, refs, o_ref, parts = refs[:count], refs[count:-2], refs[-2], refs[-1]
    tile_refs = refs[: len(refs) - begun - (rider == "cut")]
    blocks, rows, blk = parts.shape
    width = rows // 3
    at = 0
    for v_ref in v_refs:
        for i in range((blocks - 1) // count):
            v = v_ref[i, :width] if len(v_ref.shape) == 3 else v_ref[i * width : (i + 1) * width]
            high = v.astype(jnp.bfloat16)
            rest = v - high.astype(jnp.float32)
            middle = rest.astype(jnp.bfloat16)
            parts[at, 0:width, :] = high
            parts[at, width : 2 * width, :] = middle
            parts[at, 2 * width :, :] = (rest - middle.astype(jnp.float32)).astype(jnp.bfloat16)
            at += 1
    parts[at] = jnp.zeros(parts.shape[1:], jnp.bfloat16)
    o_ref[...] = refs[-1][...] if begun else jnp.zeros_like(o_ref)
    slots = place_ref.shape[0] // NS
    at = start
    for tiles_ref in tile_refs:
        for t in range(tiles_ref.shape[0]):
            slot = (own_ref[0] ^ (at // slots)) * slots + at % slots
            at += 1
            p = lax.dot_general(
                parts[source_ref[slot]],
                tiles_ref[t],
                (((1,), (0,)), ((), ())),
                preferred_element_type=jnp.float32,
            )
            place = place_ref[slot]
            to = pl.ds(pl.multiple_of(place % NS * width, width), width)
            o_ref[place // NS, to, :] += p[0:width] + p[width : 2 * width] + p[2 * width :]
    members, total, _ = o_ref.shape
    extra = total - NS * width
    for m in range(members):
        if rider == "cut":
            o_ref[m, NS * width :, :] = refs[-1][m * extra : (m + 1) * extra, :]
        if rider == "sum":
            x = [r[NS * width :, :] for r in v_refs]
            o_ref[m, NS * width :, :] = (x[0] + x[1]) + (x[2] + x[3])


def product(own, place, source, vs, tiles, width, start=0, begun=None, cut=None, add=False):
    blk = tiles[0].shape[-1]
    blocks = 4 * NS
    rider = "cut" if cut is not None else "sum" if add else None
    extra = cut.shape[0] // NM if cut is not None else vs[0].shape[0] - NS * width if add else 0
    smem = pl.BlockSpec(memory_space=pltpu.SMEM)
    vmem = pl.BlockSpec(memory_space=pltpu.VMEM)
    last = [x for x in (begun, cut) if x is not None]
    return pl.pallas_call(
        functools.partial(product_kernel, len(vs), begun is not None, rider, start),
        out_shape=jax.ShapeDtypeStruct((NM, NS * width + extra, blk), jnp.float32),
        in_specs=[smem] * 3 + [vmem] * (len(vs) + len(tiles) + len(last)),
        out_specs=vmem,
        scratch_shapes=[pltpu.VMEM((blocks + 1, 3 * width, blk), jnp.bfloat16)],
        compiler_params=GRANT,
        name="product",
    )(own.reshape(1), place, source, *vs, *tiles, *last)


def factor_solve(gram, right):
    size = gram.shape[0]
    count = size // 8

    def spread(x):
        return jnp.broadcast_to(x, (8, size))

    left = [gram[8 * r : 8 * r + 8, :] for r in range(count)]
    right = list(right)
    out = []
    for p in range(count):
        steps, rows = [], []
        for r in range(p, count):
            columns = [spread(left[r][:, 8 * p + m : 8 * p + m + 1]) for m in range(8)]
            for j in range(8):
                if r == p:
                    scale = lax.rsqrt(spread(columns[j][j : j + 1, :]))
                    others = [spread(columns[m][j : j + 1, :]) * scale for m in range(j + 1, 8)]
                    steps.append((scale, others, spread(left[r][j : j + 1, :]) * scale, spread(right[r][j : j + 1, :]) * scale))
                    rows.append(steps[j][3][0:1])
                scale, others, up, row = steps[j]
                entry = columns[j] * scale
                for m in range(j + 1, 8):
                    columns[m] = columns[m] - entry * others[m - j - 1]
                left[r] = left[r] - entry * up
                right[r] = right[r] - entry * row
        out.append(jnp.concatenate(rows, axis=0))
    return out


def factor_kernel(got_ref, o_ref):
    size = o_ref.shape[0]
    extra = size // got_ref.shape[0]
    gram = jnp.concatenate([got_ref[m, got_ref.shape[1] - extra :, :] for m in range(got_ref.shape[0])], axis=0)
    lane = lax.broadcasted_iota(jnp.int32, (8, size), 1)
    sub = lax.broadcasted_iota(jnp.int32, (8, size), 0)
    identity = [jnp.where(lane == sub + 8 * r, 1.0, 0.0) for r in range(size // 8)]
    for i, rows in enumerate(factor_solve(gram, identity)):
        o_ref[8 * i : 8 * i + 8, :] = rows


def factor(got):
    size = got.shape[2]
    return pl.pallas_call(
        factor_kernel,
        out_shape=jax.ShapeDtypeStruct((size, size), jnp.float32),
        compiler_params=GRANT,
        name="factor",
    )(got)


def fold(gram):
    half = gram.shape[0] // 2
    row = lax.broadcasted_iota(jnp.int32, (half, 2 * half), 0)
    column = lax.broadcasted_iota(jnp.int32, (half, 2 * half), 1) - half
    top, low = gram[:half], gram[half:]
    body = jnp.where((column < 0) | (row < column), low, pltpu.roll(top, half, 1))
    diagonal = jnp.sum(jnp.where(row == column, low, 0.0), axis=0, keepdims=True)
    return jnp.concatenate([body, jnp.broadcast_to(diagonal, (8, 2 * half))], axis=0)


def unfold(folded):
    half = folded.shape[1] // 2
    row = lax.broadcasted_iota(jnp.int32, (half, 2 * half), 0)
    column = lax.broadcasted_iota(jnp.int32, (half, 2 * half), 1)
    body, diagonal = folded[:half], folded[half : half + 1]
    turned = jnp.concatenate([body, jnp.zeros_like(body)], axis=0).T
    beside, below = turned[:half], turned[half:]
    first = jnp.where(row >= column, pltpu.roll(body, half, 1), below)
    top = jnp.where(column < half, first, pltpu.roll(beside, half, 1))
    column = column - half
    last = jnp.where(row == column, diagonal, pltpu.roll(below, half, 1))
    low = jnp.where((column < 0) | (row < column), body, last)
    return jnp.concatenate([top, low], axis=0)


def finish_kernel(scale, folded_ref, x_ref, o_ref):
    folded = folded_ref[0]
    for i in range(1, folded_ref.shape[0]):
        folded = folded + folded_ref[i]
    x = [x_ref[8 * r : 8 * r + 8, :] for r in range(x_ref.shape[0] // 8)]
    x = factor_solve(unfold(folded), x)
    o_ref[...] = jnp.concatenate(x, axis=0).T * scale


def finish(folded, x, scale):
    return pl.pallas_call(
        functools.partial(finish_kernel, scale),
        out_shape=jax.ShapeDtypeStruct(x.shape[::-1], jnp.float32),
        compiler_params=GRANT,
        name="finish",
    )(folded, x)


def join(own, refs, x_ref):
    blk = refs[0].shape[1]
    width = x_ref.shape[0] // NS
    for i, r in enumerate(refs):
        rows = pl.ds(pl.multiple_of((own ^ i) * width, width), width)
        for b in range(NS):
            x_ref[rows, b * blk : (b + 1) * blk] = r[b * width : (b + 1) * width]


def inner(x):
    return lax.dot_general(x, x, (((1,), (1,)), ((), ())), precision=HIGH, preferred_element_type=jnp.float32)


def gram_kernel(own_ref, *refs):
    o_ref, x_ref = refs[-2:]
    join(own_ref[0], refs[:-2], x_ref)
    o_ref[...] = inner(x_ref[...])


def gram(own, slices):
    width, blk = slices[0].shape
    blocks = NS
    vmem = pl.BlockSpec(memory_space=pltpu.VMEM)
    return pl.pallas_call(
        gram_kernel,
        out_shape=jax.ShapeDtypeStruct((width, width), jnp.float32),
        in_specs=[pl.BlockSpec(memory_space=pltpu.SMEM)] + [vmem] * len(slices),
        scratch_shapes=[pltpu.VMEM((width, blocks * blk), jnp.float32)],
        compiler_params=GRANT,
        name="gram",
    )(own.reshape(1), *slices)


def normal_kernel(own_ref, inverse_ref, *refs):
    o_ref, gram_ref, x_ref, all_ref = refs[-4:]
    join(own_ref[0], refs[:-4], x_ref)
    y = jnp.dot(inverse_ref[...], x_ref[...], precision=HIGH, preferred_element_type=jnp.float32)
    gram_ref[...] = fold(inner(y))
    blk = o_ref.shape[1]
    for i in range(all_ref.shape[0]):
        all_ref[i] = y[:, i * blk : (i + 1) * blk]
    o_ref[...] = all_ref[own_ref[0]]


def normal(own, inverse, slices):
    width, blk = slices[0].shape
    blocks = NS
    vmem = pl.BlockSpec(memory_space=pltpu.VMEM)
    return pl.pallas_call(
        normal_kernel,
        out_shape=(
            jax.ShapeDtypeStruct((width, blk), jnp.float32),
            jax.ShapeDtypeStruct((width // 2 + 8, width), jnp.float32),
        ),
        in_specs=[pl.BlockSpec(memory_space=pltpu.SMEM)] + [vmem] * (1 + len(slices)),
        scratch_shapes=[
            pltpu.VMEM((width, blocks * blk), jnp.float32),
            pltpu.VMEM((blocks, width, blk), jnp.float32),
        ],
        compiler_params=GRANT,
        name="normal",
    )(own.reshape(1), inverse, *slices)


def ends_kernel(bounds_ref, centre_ref, half_ref):
    centre_ref[...] = jnp.full(centre_ref.shape, (bounds_ref[0] + bounds_ref[1]) / 2.0)
    half_ref[...] = jnp.full(half_ref.shape, (bounds_ref[1] - bounds_ref[0]) / 2.0)


def ends(bounds, width):
    row = jax.ShapeDtypeStruct((1, width), jnp.float32)
    return pl.pallas_call(
        ends_kernel,
        out_shape=(row, row),
        in_specs=[pl.BlockSpec(memory_space=pltpu.SMEM)],
        compiler_params=GRANT,
        name="ends",
    )(bounds)


def on_device(start_block, tiles, tile_rows, tile_cols, bounds):
    blk = tiles.shape[1]
    centre, half = ends(bounds, blk)
    width = start_block.shape[1]
    total_rows = blk * 2 ** len(AXES)
    own = 0
    for name in SPLIT:
        own = own * 2 + lax.axis_index(name)
    own_row = 2 * lax.axis_index("ylo") + lax.axis_index("core")
    tie = lax.optimization_barrier

    start_block, centre, half = tie((start_block, centre, half))
    slots = tile_rows.shape[0]
    notes = jnp.pad(jnp.stack([tile_rows, tile_cols]).astype(jnp.float32), ((0, 6), (0, blk - slots)))
    slices = start_block.T.reshape(NS, width // NS, blk)
    slices = jnp.concatenate([slices, jnp.broadcast_to(notes, (NS, *notes.shape))], axis=1)
    got = exchange(jnp.broadcast_to(slices, (4, *slices.shape)).reshape(4 * NS, *slices.shape[1:]), ROW + SPLIT)
    tile_sets, got = share_tiles(tiles, got)
    begun = got
    got = lax.dynamic_index_in_dim(got.reshape(4, NS, *got.shape[1:]), own_row, 0, keepdims=False)
    current = got[:, : width // NS].reshape(width, blk)
    all_rows, all_cols = (got[:, width // NS + i, :slots].astype(jnp.int32) for i in range(2))
    live = all_rows >= 0
    member = jnp.arange(NS, dtype=jnp.int32)[:, None]
    source = jnp.where(live, (all_cols ^ own_row) * NS + member, 4 * NS).reshape(-1)
    source_begun = jnp.where(live, all_cols * NS + member, 4 * NS).reshape(-1)
    place = jnp.where(live, digits(all_rows, SCATTER) * NS + digits(all_rows, SPLIT), 0).reshape(-1)
    early = sum(t.shape[0] for t in tile_sets[:-1])

    part = width // NS

    def multiply(v, others, **riders):
        return exchange(product(own, place, source, [v, *others], tile_sets, part, **riders), SCATTER)

    def multiply_first():
        prods = product(own, place, source_begun, [begun], tile_sets[:-1], part)
        return exchange(product(own, place, source_begun, [begun], tile_sets[-1:], part, early, prods), SCATTER)

    def add_up(got):
        return jnp.sum(got, axis=0)

    def add_three(x, others):
        return (x + others[0]) + (others[1] + others[2])

    current, centre, half = tie((current, centre, half))
    first = (add_up(multiply_first()) - centre * current) / half
    second = 2.0 * (add_up(multiply(first, three(first, ROW))) - centre * first) / half - current
    third = 2.0 * (add_up(multiply(second, three(second, ROW))) - centre * second) / half - first

    current = third
    first = (add_up(multiply(current, three(current, ROW))) - centre * current) / half
    slices = three(current, SPLIT)
    others = three(first, ROW)
    got = add_up(multiply(first, others, cut=gram(own, [current, *slices])))
    second = 2.0 * (got[:width] - centre * first) / half - current
    second = jnp.concatenate([second, got[width:]], axis=0)
    got = multiply(second, three(second, ROW), add=True)
    third = 2.0 * (add_up(got[:, :width]) - centre * second[:width]) / half - first
    inverse = factor(got)

    block, local = normal(own, inverse, [third, *three(third, SPLIT)])
    local = add_three(local, three(local, ROW))
    folded = exchange(jnp.broadcast_to(local, (NM, *local.shape)), SCATTER)
    return finish(folded, block, math.sqrt(total_rows))


def solution(mesh):
    fine = Mesh(mesh.devices.reshape((2,) * len(AXES)), AXES)
    return jax.shard_map(
        on_device,
        mesh=fine,
        in_specs=(P(AXES, None), P(AXES, None, None), P(AXES), P(AXES), P()),
        out_specs=P(AXES, None),
        check_vma=False,
    )
```

```python
import functools
import math

import jax
import jax.numpy as jnp
from jax import lax
from jax.experimental import pallas as pl
from jax.experimental.pallas import tpu as pltpu
from jax.sharding import Mesh
from jax.sharding import PartitionSpec as P

ITERS = 2
HIGH = lax.Precision.HIGHEST
AXES = ("ylo", "core", "zhi", "zlo", "xhi", "xlo", "yhi")
ROW = ("ylo", "core")
COL = ("zhi", "zlo", "xhi", "xlo", "yhi")
SPLIT = ("xhi", "yhi")
SCATTER = ("xlo", "zlo", "zhi")
NS = 2 ** len(SPLIT)
NM = 2 ** len(SCATTER)
GRANT = pltpu.CompilerParams(vmem_limit_bytes=16 * 2**20)


def digits(index, names):
    out = 0
    for name in names:
        shift = len(COL) - 1 - COL.index(name)
        out = out * 2 + ((index >> shift) & 1)
    return out


def swap(x, name):
    return lax.ppermute(x, name, [(0, 1), (1, 0)])


def three(x, names):
    return [swap(x, names[1]), swap(x, names[0]), lax.ppermute(x, names, [(i, i ^ 3) for i in range(4)])]


def exchange(x, names):
    if not names:
        return x
    return lax.all_to_all(x, names, 0, 0, tiled=True)


def turn(tile):
    size = tile.shape[0]
    row = lax.broadcasted_iota(jnp.int32, (size, size), 0)
    column = lax.broadcasted_iota(jnp.int32, (size, size), 1)
    identity = jnp.where(row == column, 1.0, 0.0).astype(tile.dtype)
    return lax.dot_general(identity, tile, (((1,), (1,)), ((), ())), preferred_element_type=jnp.float32)


def widen_kernel(tiles_ref, a_ref, b_ref):
    slots, blk, _ = tiles_ref.shape
    half = slots // 2
    for i in range(half):
        a_ref[i * blk : (i + 1) * blk, :] = turn(tiles_ref[i])
        b_ref[i * blk : (i + 1) * blk, :] = turn(tiles_ref[half + i])


def widen(tiles):
    slots, blk, _ = tiles.shape
    wide = jax.ShapeDtypeStruct((slots // 2 * blk, blk), jnp.float32)
    return pl.pallas_call(
        widen_kernel,
        out_shape=(wide, wide),
        compiler_params=GRANT,
        name="widen",
    )(tiles)


def turn_kernel(tiles_ref, o_ref):
    for i in range(tiles_ref.shape[0]):
        o_ref[i] = turn(tiles_ref[i]).astype(o_ref.dtype)


def turn_all(tiles):
    return pl.pallas_call(
        turn_kernel,
        out_shape=jax.ShapeDtypeStruct(tiles.shape, tiles.dtype),
        compiler_params=GRANT,
        name="turn",
    )(tiles)


def pack_kernel(*refs):
    o_ref = refs[-1]
    _, step, blk, _ = o_ref.shape
    for i, r in enumerate(refs[:-1]):
        for k in range(step):
            o_ref[i, k] = r[k * blk : (k + 1) * blk, :].astype(o_ref.dtype)


def pack(parts, slots):
    blk = parts[0].shape[1]
    step = 4
    spec = pl.BlockSpec((step * blk, blk), lambda i: (i, 0))
    return pl.pallas_call(
        pack_kernel,
        grid=(slots // step,),
        out_shape=jax.ShapeDtypeStruct((len(parts), slots, blk, blk), jnp.bfloat16),
        in_specs=[spec] * len(parts),
        out_specs=pl.BlockSpec((len(parts), step, blk, blk), lambda i: (0, i, 0, 0)),
        compiler_params=GRANT,
        name="pack",
    )(*parts).reshape(-1, blk, blk)


def share_tiles(tiles, small):
    half = tiles.shape[0] // 2
    a, b = widen(tiles)
    a_y, b_x = swap(a, "yhi"), swap(b, "xhi")
    a_x, b_y = swap(a, "xhi"), swap(b, "yhi")
    a_xy, b_xy = swap(a_y, "xhi"), swap(b_x, "yhi")
    _, tiles = lax.optimization_barrier((a_x, tiles))
    return (turn_all(tiles), pack([a_y, b_y, a_x, b_x], half), pack([a_xy, b_xy], half)), small


def product_kernel(count, begun, rider, start, own_ref, place_ref, source_ref, *refs):
    v_refs, refs, o_ref, parts = refs[:count], refs[count:-2], refs[-2], refs[-1]
    tile_refs = refs[: len(refs) - begun - (rider == "cut")]
    blocks, rows, blk = parts.shape
    width = rows // 3
    at = 0
    for v_ref in v_refs:
        for i in range((blocks - 1) // count):
            v = v_ref[i, :width] if len(v_ref.shape) == 3 else v_ref[i * width : (i + 1) * width]
            high = v.astype(jnp.bfloat16)
            rest = v - high.astype(jnp.float32)
            middle = rest.astype(jnp.bfloat16)
            parts[at, 0:width, :] = high
            parts[at, width : 2 * width, :] = middle
            parts[at, 2 * width :, :] = (rest - middle.astype(jnp.float32)).astype(jnp.bfloat16)
            at += 1
    parts[at] = jnp.zeros(parts.shape[1:], jnp.bfloat16)
    o_ref[...] = refs[-1][...] if begun else jnp.zeros_like(o_ref)
    slots = place_ref.shape[0] // NS
    at = start
    for tiles_ref in tile_refs:
        for t in range(tiles_ref.shape[0]):
            slot = (own_ref[0] ^ (at // slots)) * slots + at % slots
            at += 1
            p = lax.dot_general(
                parts[source_ref[slot]],
                tiles_ref[t],
                (((1,), (0,)), ((), ())),
                preferred_element_type=jnp.float32,
            )
            place = place_ref[slot]
            to = pl.ds(pl.multiple_of(place % NS * width, width), width)
            o_ref[place // NS, to, :] += p[0:width] + p[width : 2 * width] + p[2 * width :]
    members, total, _ = o_ref.shape
    extra = total - NS * width
    for m in range(members):
        if rider == "cut":
            o_ref[m, NS * width :, :] = refs[-1][m * extra : (m + 1) * extra, :]
        if rider == "sum":
            x = [r[NS * width :, :] for r in v_refs]
            o_ref[m, NS * width :, :] = (x[0] + x[1]) + (x[2] + x[3])


def product(own, place, source, vs, tiles, width, start=0, begun=None, cut=None, add=False):
    blk = tiles[0].shape[-1]
    blocks = 4 * NS
    rider = "cut" if cut is not None else "sum" if add else None
    extra = cut.shape[0] // NM if cut is not None else vs[0].shape[0] - NS * width if add else 0
    smem = pl.BlockSpec(memory_space=pltpu.SMEM)
    vmem = pl.BlockSpec(memory_space=pltpu.VMEM)
    last = [x for x in (begun, cut) if x is not None]
    return pl.pallas_call(
        functools.partial(product_kernel, len(vs), begun is not None, rider, start),
        out_shape=jax.ShapeDtypeStruct((NM, NS * width + extra, blk), jnp.float32),
        in_specs=[smem] * 3 + [vmem] * (len(vs) + len(tiles) + len(last)),
        out_specs=vmem,
        scratch_shapes=[pltpu.VMEM((blocks + 1, 3 * width, blk), jnp.bfloat16)],
        compiler_params=GRANT,
        name="product",
    )(own.reshape(1), place, source, *vs, *tiles, *last)


def factor_solve(gram, right):
    size = gram.shape[0]
    count = size // 8

    def spread(x):
        return jnp.broadcast_to(x, (8, size))

    left = [gram[8 * r : 8 * r + 8, :] for r in range(count)]
    right = list(right)
    out = []
    for p in range(count):
        steps, rows = [], []
        for r in range(p, count):
            columns = [spread(left[r][:, 8 * p + m : 8 * p + m + 1]) for m in range(8)]
            for j in range(8):
                if r == p:
                    scale = lax.rsqrt(spread(columns[j][j : j + 1, :]))
                    others = [spread(columns[m][j : j + 1, :]) * scale for m in range(j + 1, 8)]
                    steps.append((scale, others, spread(left[r][j : j + 1, :]) * scale, spread(right[r][j : j + 1, :]) * scale))
                    rows.append(steps[j][3][0:1])
                scale, others, up, row = steps[j]
                entry = columns[j] * scale
                for m in range(j + 1, 8):
                    columns[m] = columns[m] - entry * others[m - j - 1]
                left[r] = left[r] - entry * up
                right[r] = right[r] - entry * row
        out.append(jnp.concatenate(rows, axis=0))
    return out


def factor_kernel(got_ref, o_ref):
    size = o_ref.shape[0]
    extra = size // got_ref.shape[0]
    gram = jnp.concatenate([got_ref[m, got_ref.shape[1] - extra :, :] for m in range(got_ref.shape[0])], axis=0)
    lane = lax.broadcasted_iota(jnp.int32, (8, size), 1)
    sub = lax.broadcasted_iota(jnp.int32, (8, size), 0)
    identity = [jnp.where(lane == sub + 8 * r, 1.0, 0.0) for r in range(size // 8)]
    for i, rows in enumerate(factor_solve(gram, identity)):
        o_ref[8 * i : 8 * i + 8, :] = rows


def factor(got):
    size = got.shape[2]
    return pl.pallas_call(
        factor_kernel,
        out_shape=jax.ShapeDtypeStruct((size, size), jnp.float32),
        compiler_params=GRANT,
        name="factor",
    )(got)


def fold(gram):
    half = gram.shape[0] // 2
    row = lax.broadcasted_iota(jnp.int32, (half, 2 * half), 0)
    column = lax.broadcasted_iota(jnp.int32, (half, 2 * half), 1) - half
    top, low = gram[:half], gram[half:]
    body = jnp.where((column < 0) | (row < column), low, pltpu.roll(top, half, 1))
    diagonal = jnp.sum(jnp.where(row == column, low, 0.0), axis=0, keepdims=True)
    return jnp.concatenate([body, jnp.broadcast_to(diagonal, (8, 2 * half))], axis=0)


def unfold(folded):
    half = folded.shape[1] // 2
    row = lax.broadcasted_iota(jnp.int32, (half, 2 * half), 0)
    column = lax.broadcasted_iota(jnp.int32, (half, 2 * half), 1)
    body, diagonal = folded[:half], folded[half : half + 1]
    turned = jnp.concatenate([body, jnp.zeros_like(body)], axis=0).T
    beside, below = turned[:half], turned[half:]
    first = jnp.where(row >= column, pltpu.roll(body, half, 1), below)
    top = jnp.where(column < half, first, pltpu.roll(beside, half, 1))
    column = column - half
    last = jnp.where(row == column, diagonal, pltpu.roll(below, half, 1))
    low = jnp.where((column < 0) | (row < column), body, last)
    return jnp.concatenate([top, low], axis=0)


def finish_kernel(scale, folded_ref, x_ref, o_ref):
    folded = folded_ref[0]
    for i in range(1, folded_ref.shape[0]):
        folded = folded + folded_ref[i]
    x = [x_ref[8 * r : 8 * r + 8, :] for r in range(x_ref.shape[0] // 8)]
    x = factor_solve(unfold(folded), x)
    o_ref[...] = jnp.concatenate(x, axis=0).T * scale


def finish(folded, x, scale):
    return pl.pallas_call(
        functools.partial(finish_kernel, scale),
        out_shape=jax.ShapeDtypeStruct(x.shape[::-1], jnp.float32),
        compiler_params=GRANT,
        name="finish",
    )(folded, x)


def join(own, refs, x_ref):
    blk = refs[0].shape[1]
    width = x_ref.shape[0] // NS
    for i, r in enumerate(refs):
        rows = pl.ds(pl.multiple_of((own ^ i) * width, width), width)
        for b in range(NS):
            x_ref[rows, b * blk : (b + 1) * blk] = r[b * width : (b + 1) * width]


def inner(x):
    return lax.dot_general(x, x, (((1,), (1,)), ((), ())), precision=HIGH, preferred_element_type=jnp.float32)


def gram_kernel(own_ref, *refs):
    o_ref, x_ref = refs[-2:]
    join(own_ref[0], refs[:-2], x_ref)
    o_ref[...] = inner(x_ref[...])


def gram(own, slices):
    width, blk = slices[0].shape
    blocks = NS
    vmem = pl.BlockSpec(memory_space=pltpu.VMEM)
    return pl.pallas_call(
        gram_kernel,
        out_shape=jax.ShapeDtypeStruct((width, width), jnp.float32),
        in_specs=[pl.BlockSpec(memory_space=pltpu.SMEM)] + [vmem] * len(slices),
        scratch_shapes=[pltpu.VMEM((width, blocks * blk), jnp.float32)],
        compiler_params=GRANT,
        name="gram",
    )(own.reshape(1), *slices)


def normal_kernel(own_ref, inverse_ref, *refs):
    o_ref, gram_ref, x_ref, all_ref = refs[-4:]
    join(own_ref[0], refs[:-4], x_ref)
    y = jnp.dot(inverse_ref[...], x_ref[...], precision=HIGH, preferred_element_type=jnp.float32)
    gram_ref[...] = fold(inner(y))
    blk = o_ref.shape[1]
    for i in range(all_ref.shape[0]):
        all_ref[i] = y[:, i * blk : (i + 1) * blk]
    o_ref[...] = all_ref[own_ref[0]]


def normal(own, inverse, slices):
    width, blk = slices[0].shape
    blocks = NS
    vmem = pl.BlockSpec(memory_space=pltpu.VMEM)
    return pl.pallas_call(
        normal_kernel,
        out_shape=(
            jax.ShapeDtypeStruct((width, blk), jnp.float32),
            jax.ShapeDtypeStruct((width // 2 + 8, width), jnp.float32),
        ),
        in_specs=[pl.BlockSpec(memory_space=pltpu.SMEM)] + [vmem] * (1 + len(slices)),
        scratch_shapes=[
            pltpu.VMEM((width, blocks * blk), jnp.float32),
            pltpu.VMEM((blocks, width, blk), jnp.float32),
        ],
        compiler_params=GRANT,
        name="normal",
    )(own.reshape(1), inverse, *slices)


def ends_kernel(bounds_ref, centre_ref, half_ref):
    centre_ref[...] = jnp.full(centre_ref.shape, (bounds_ref[0] + bounds_ref[1]) / 2.0)
    half_ref[...] = jnp.full(half_ref.shape, (bounds_ref[1] - bounds_ref[0]) / 2.0)


def ends(bounds, width):
    row = jax.ShapeDtypeStruct((1, width), jnp.float32)
    return pl.pallas_call(
        ends_kernel,
        out_shape=(row, row),
        in_specs=[pl.BlockSpec(memory_space=pltpu.SMEM)],
        compiler_params=GRANT,
        name="ends",
    )(bounds)


def on_device(start_block, tiles, tile_rows, tile_cols, bounds):
    blk = tiles.shape[1]
    centre, half = ends(bounds, blk)
    width = start_block.shape[1]
    total_rows = blk * 2 ** len(AXES)
    own = 0
    for name in SPLIT:
        own = own * 2 + lax.axis_index(name)
    own_row = 2 * lax.axis_index("ylo") + lax.axis_index("core")
    tie = lax.optimization_barrier

    start_block, centre, half = tie((start_block, centre, half))
    slots = tile_rows.shape[0]
    notes = jnp.pad(jnp.stack([tile_rows, tile_cols]).astype(jnp.float32), ((0, 6), (0, blk - slots)))
    slices = start_block.T.reshape(NS, width // NS, blk)
    slices = jnp.concatenate([slices, jnp.broadcast_to(notes, (NS, *notes.shape))], axis=1)
    near = exchange(jnp.concatenate([slices, slices], axis=0), ("ylo",) + SPLIT)
    tile_sets, near = share_tiles(tiles, near)
    begun = [near, swap(near, "core")]
    got = lax.dynamic_index_in_dim(near.reshape(2, NS, *near.shape[1:]), lax.axis_index("ylo"), 0, keepdims=False)
    current = got[:, : width // NS].reshape(width, blk)
    all_rows, all_cols = (got[:, width // NS + i, :slots].astype(jnp.int32) for i in range(2))
    live = all_rows >= 0
    member = jnp.arange(NS, dtype=jnp.int32)[:, None]
    source = jnp.where(live, (all_cols ^ own_row) * NS + member, 4 * NS).reshape(-1)
    column = (all_cols ^ lax.axis_index("core")) % 2 * 2 + all_cols // 2
    source_begun = jnp.where(live, column * NS + member, 4 * NS).reshape(-1)
    place = jnp.where(live, digits(all_rows, SCATTER) * NS + digits(all_rows, SPLIT), 0).reshape(-1)
    early = sum(t.shape[0] for t in tile_sets[:-1])

    part = width // NS

    def multiply(v, others, **riders):
        return exchange(product(own, place, source, [v, *others], tile_sets, part, **riders), SCATTER)

    def multiply_first(small):
        prods = product(own, place, source_begun, begun, tile_sets[:-1], part)
        prods, small = tie((prods, small))
        return small, exchange(product(own, place, source_begun, begun, tile_sets[-1:], part, early, prods), SCATTER)

    def add_up(got):
        return jnp.sum(got, axis=0)

    def add_three(x, others):
        return (x + others[0]) + (others[1] + others[2])

    (current, centre, half), got = multiply_first((current, centre, half))
    first = (add_up(got) - centre * current) / half
    second = 2.0 * (add_up(multiply(first, three(first, ROW))) - centre * first) / half - current
    third = 2.0 * (add_up(multiply(second, three(second, ROW))) - centre * second) / half - first

    current = third
    first = (add_up(multiply(current, three(current, ROW))) - centre * current) / half
    slices = three(current, SPLIT)
    others = three(first, ROW)
    got = add_up(multiply(first, others, cut=gram(own, [current, *slices])))
    second = 2.0 * (got[:width] - centre * first) / half - current
    second = jnp.concatenate([second, got[width:]], axis=0)
    got = multiply(second, three(second, ROW), add=True)
    third = 2.0 * (add_up(got[:, :width]) - centre * second[:width]) / half - first
    inverse = factor(got)

    block, local = normal(own, inverse, [third, *three(third, SPLIT)])
    local = add_three(local, three(local, ROW))
    folded = exchange(jnp.broadcast_to(local, (NM, *local.shape)), SCATTER)
    return finish(folded, block, math.sqrt(total_rows))


def solution(mesh):
    fine = Mesh(mesh.devices.reshape((2,) * len(AXES)), AXES)
    return jax.shard_map(
        on_device,
        mesh=fine,
        in_specs=(P(AXES, None), P(AXES, None, None), P(AXES), P(AXES), P()),
        out_specs=P(AXES, None),
        check_vma=False,
    )
```

```python
import functools
import math

import jax
import jax.numpy as jnp
from jax import lax
from jax.experimental import pallas as pl
from jax.experimental.pallas import tpu as pltpu
from jax.sharding import Mesh
from jax.sharding import PartitionSpec as P

ITERS = 2
HIGH = lax.Precision.HIGHEST
AXES = ("ylo", "core", "zhi", "zlo", "xhi", "xlo", "yhi")
ROW = ("ylo", "core")
COL = ("zhi", "zlo", "xhi", "xlo", "yhi")
SPLIT = ("xhi", "yhi")
SCATTER = ("xlo", "zlo", "zhi")
NS = 2 ** len(SPLIT)
NM = 2 ** len(SCATTER)
GRANT = pltpu.CompilerParams(vmem_limit_bytes=16 * 2**20)


def digits(index, names):
    out = 0
    for name in names:
        shift = len(COL) - 1 - COL.index(name)
        out = out * 2 + ((index >> shift) & 1)
    return out


def swap(x, name):
    return lax.ppermute(x, name, [(0, 1), (1, 0)])


def three(x, names):
    return [lax.ppermute(x, names, [(i, i ^ 3) for i in range(4)]), swap(x, names[0]), swap(x, names[1])]


def exchange(x, names):
    if not names:
        return x
    return lax.all_to_all(x, names, 0, 0, tiled=True)


def turn(tile):
    size = tile.shape[0]
    row = lax.broadcasted_iota(jnp.int32, (size, size), 0)
    column = lax.broadcasted_iota(jnp.int32, (size, size), 1)
    identity = jnp.where(row == column, 1.0, 0.0).astype(tile.dtype)
    return lax.dot_general(identity, tile, (((1,), (1,)), ((), ())), preferred_element_type=jnp.float32)


def widen_kernel(tiles_ref, a_ref, b_ref):
    slots, blk, _ = tiles_ref.shape
    half = slots // 2
    for i in range(half):
        a_ref[i * blk : (i + 1) * blk, :] = turn(tiles_ref[i])
        b_ref[i * blk : (i + 1) * blk, :] = turn(tiles_ref[half + i])


def widen(tiles):
    slots, blk, _ = tiles.shape
    wide = jax.ShapeDtypeStruct((slots // 2 * blk, blk), jnp.float32)
    return pl.pallas_call(
        widen_kernel,
        out_shape=(wide, wide),
        compiler_params=GRANT,
        name="widen",
    )(tiles)


def turn_kernel(tiles_ref, o_ref):
    for i in range(tiles_ref.shape[0]):
        o_ref[i] = turn(tiles_ref[i]).astype(o_ref.dtype)


def turn_all(tiles):
    return pl.pallas_call(
        turn_kernel,
        out_shape=jax.ShapeDtypeStruct(tiles.shape, tiles.dtype),
        compiler_params=GRANT,
        name="turn",
    )(tiles)


def pack_kernel(*refs):
    o_ref = refs[-1]
    _, step, blk, _ = o_ref.shape
    for i, r in enumerate(refs[:-1]):
        for k in range(step):
            o_ref[i, k] = r[k * blk : (k + 1) * blk, :].astype(o_ref.dtype)


def pack(parts, slots):
    blk = parts[0].shape[1]
    step = 4
    spec = pl.BlockSpec((step * blk, blk), lambda i: (i, 0))
    return pl.pallas_call(
        pack_kernel,
        grid=(slots // step,),
        out_shape=jax.ShapeDtypeStruct((len(parts), slots, blk, blk), jnp.bfloat16),
        in_specs=[spec] * len(parts),
        out_specs=pl.BlockSpec((len(parts), step, blk, blk), lambda i: (0, i, 0, 0)),
        compiler_params=GRANT,
        name="pack",
    )(*parts).reshape(-1, blk, blk)


def share_tiles(tiles, small):
    half = tiles.shape[0] // 2
    a, b = widen(tiles)
    a_y, b_x = swap(a, "yhi"), swap(b, "xhi")
    a_x, b_y = swap(a, "xhi"), swap(b, "yhi")
    a_xy, b_xy = swap(a_y, "xhi"), swap(b_x, "yhi")
    _, tiles = lax.optimization_barrier((a_x, tiles))
    return (turn_all(tiles), pack([a_y, b_y, a_x, b_x], half), pack([a_xy, b_xy], half)), small


def product_kernel(count, begun, rider, start, own_ref, place_ref, source_ref, *refs):
    v_refs, refs, o_ref, parts = refs[:count], refs[count:-2], refs[-2], refs[-1]
    tile_refs = refs[: len(refs) - begun - (rider == "cut")]
    blocks, rows, blk = parts.shape
    width = rows // 3
    at = 0
    for v_ref in v_refs:
        for i in range((blocks - 1) // count):
            v = v_ref[i, :width] if len(v_ref.shape) == 3 else v_ref[i * width : (i + 1) * width]
            high = v.astype(jnp.bfloat16)
            rest = v - high.astype(jnp.float32)
            middle = rest.astype(jnp.bfloat16)
            parts[at, 0:width, :] = high
            parts[at, width : 2 * width, :] = middle
            parts[at, 2 * width :, :] = (rest - middle.astype(jnp.float32)).astype(jnp.bfloat16)
            at += 1
    parts[at] = jnp.zeros(parts.shape[1:], jnp.bfloat16)
    o_ref[...] = refs[-1][...] if begun else jnp.zeros_like(o_ref)
    slots = place_ref.shape[0] // NS
    at = start
    for tiles_ref in tile_refs:
        for t in range(tiles_ref.shape[0]):
            slot = (own_ref[0] ^ (at // slots)) * slots + at % slots
            at += 1
            p = lax.dot_general(
                parts[source_ref[slot]],
                tiles_ref[t],
                (((1,), (0,)), ((), ())),
                preferred_element_type=jnp.float32,
            )
            place = place_ref[slot]
            to = pl.ds(pl.multiple_of(place % NS * width, width), width)
            o_ref[place // NS, to, :] += p[0:width] + p[width : 2 * width] + p[2 * width :]
    members, total, _ = o_ref.shape
    extra = total - NS * width
    for m in range(members):
        if rider == "cut":
            o_ref[m, NS * width :, :] = refs[-1][m * extra : (m + 1) * extra, :]
        if rider == "sum":
            x = [r[NS * width :, :] for r in v_refs]
            o_ref[m, NS * width :, :] = (x[0] + x[1]) + (x[2] + x[3])


def product(own, place, source, vs, tiles, width, start=0, begun=None, cut=None, add=False):
    blk = tiles[0].shape[-1]
    blocks = 4 * NS
    rider = "cut" if cut is not None else "sum" if add else None
    extra = cut.shape[0] // NM if cut is not None else vs[0].shape[0] - NS * width if add else 0
    smem = pl.BlockSpec(memory_space=pltpu.SMEM)
    vmem = pl.BlockSpec(memory_space=pltpu.VMEM)
    last = [x for x in (begun, cut) if x is not None]
    return pl.pallas_call(
        functools.partial(product_kernel, len(vs), begun is not None, rider, start),
        out_shape=jax.ShapeDtypeStruct((NM, NS * width + extra, blk), jnp.float32),
        in_specs=[smem] * 3 + [vmem] * (len(vs) + len(tiles) + len(last)),
        out_specs=vmem,
        scratch_shapes=[pltpu.VMEM((blocks + 1, 3 * width, blk), jnp.bfloat16)],
        compiler_params=GRANT,
        name="product",
    )(own.reshape(1), place, source, *vs, *tiles, *last)


def factor_solve(gram, right):
    size = gram.shape[0]
    count = size // 8

    def spread(x):
        return jnp.broadcast_to(x, (8, size))

    left = [gram[8 * r : 8 * r + 8, :] for r in range(count)]
    right = list(right)
    out = []
    for p in range(count):
        steps, rows = [], []
        for r in range(p, count):
            columns = [spread(left[r][:, 8 * p + m : 8 * p + m + 1]) for m in range(8)]
            for j in range(8):
                if r == p:
                    scale = lax.rsqrt(spread(columns[j][j : j + 1, :]))
                    others = [spread(columns[m][j : j + 1, :]) * scale for m in range(j + 1, 8)]
                    steps.append((scale, others, spread(left[r][j : j + 1, :]) * scale, spread(right[r][j : j + 1, :]) * scale))
                    rows.append(steps[j][3][0:1])
                scale, others, up, row = steps[j]
                entry = columns[j] * scale
                for m in range(j + 1, 8):
                    columns[m] = columns[m] - entry * others[m - j - 1]
                left[r] = left[r] - entry * up
                right[r] = right[r] - entry * row
        out.append(jnp.concatenate(rows, axis=0))
    return out


def factor_kernel(got_ref, o_ref):
    size = o_ref.shape[0]
    extra = size // got_ref.shape[0]
    gram = jnp.concatenate([got_ref[m, got_ref.shape[1] - extra :, :] for m in range(got_ref.shape[0])], axis=0)
    lane = lax.broadcasted_iota(jnp.int32, (8, size), 1)
    sub = lax.broadcasted_iota(jnp.int32, (8, size), 0)
    identity = [jnp.where(lane == sub + 8 * r, 1.0, 0.0) for r in range(size // 8)]
    for i, rows in enumerate(factor_solve(gram, identity)):
        o_ref[8 * i : 8 * i + 8, :] = rows


def factor(got):
    size = got.shape[2]
    return pl.pallas_call(
        factor_kernel,
        out_shape=jax.ShapeDtypeStruct((size, size), jnp.float32),
        compiler_params=GRANT,
        name="factor",
    )(got)


def fold(gram):
    half = gram.shape[0] // 2
    row = lax.broadcasted_iota(jnp.int32, (half, 2 * half), 0)
    column = lax.broadcasted_iota(jnp.int32, (half, 2 * half), 1) - half
    top, low = gram[:half], gram[half:]
    body = jnp.where((column < 0) | (row < column), low, pltpu.roll(top, half, 1))
    diagonal = jnp.sum(jnp.where(row == column, low, 0.0), axis=0, keepdims=True)
    return jnp.concatenate([body, jnp.broadcast_to(diagonal, (8, 2 * half))], axis=0)


def unfold(folded):
    half = folded.shape[1] // 2
    row = lax.broadcasted_iota(jnp.int32, (half, 2 * half), 0)
    column = lax.broadcasted_iota(jnp.int32, (half, 2 * half), 1)
    body, diagonal = folded[:half], folded[half : half + 1]
    turned = jnp.concatenate([body, jnp.zeros_like(body)], axis=0).T
    beside, below = turned[:half], turned[half:]
    first = jnp.where(row >= column, pltpu.roll(body, half, 1), below)
    top = jnp.where(column < half, first, pltpu.roll(beside, half, 1))
    column = column - half
    last = jnp.where(row == column, diagonal, pltpu.roll(below, half, 1))
    low = jnp.where((column < 0) | (row < column), body, last)
    return jnp.concatenate([top, low], axis=0)


def finish_kernel(scale, folded_ref, x_ref, o_ref):
    folded = folded_ref[0]
    for i in range(1, folded_ref.shape[0]):
        folded = folded + folded_ref[i]
    x = [x_ref[8 * r : 8 * r + 8, :] for r in range(x_ref.shape[0] // 8)]
    x = factor_solve(unfold(folded), x)
    o_ref[...] = jnp.concatenate(x, axis=0).T * scale


def finish(folded, x, scale):
    return pl.pallas_call(
        functools.partial(finish_kernel, scale),
        out_shape=jax.ShapeDtypeStruct(x.shape[::-1], jnp.float32),
        compiler_params=GRANT,
        name="finish",
    )(folded, x)


def join(own, refs, x_ref):
    blk = refs[0].shape[1]
    width = x_ref.shape[0] // NS
    for i, r in enumerate(refs):
        rows = pl.ds(pl.multiple_of((own ^ (4 - i) % 4) * width, width), width)
        for b in range(NS):
            x_ref[rows, b * blk : (b + 1) * blk] = r[b * width : (b + 1) * width]


def inner(x):
    return lax.dot_general(x, x, (((1,), (1,)), ((), ())), precision=HIGH, preferred_element_type=jnp.float32)


def gram_kernel(own_ref, *refs):
    o_ref, x_ref = refs[-2:]
    join(own_ref[0], refs[:-2], x_ref)
    o_ref[...] = inner(x_ref[...])


def gram(own, slices):
    width, blk = slices[0].shape
    blocks = NS
    vmem = pl.BlockSpec(memory_space=pltpu.VMEM)
    return pl.pallas_call(
        gram_kernel,
        out_shape=jax.ShapeDtypeStruct((width, width), jnp.float32),
        in_specs=[pl.BlockSpec(memory_space=pltpu.SMEM)] + [vmem] * len(slices),
        scratch_shapes=[pltpu.VMEM((width, blocks * blk), jnp.float32)],
        compiler_params=GRANT,
        name="gram",
    )(own.reshape(1), *slices)


def normal_kernel(own_ref, inverse_ref, *refs):
    o_ref, gram_ref, x_ref, all_ref = refs[-4:]
    join(own_ref[0], refs[:-4], x_ref)
    y = jnp.dot(inverse_ref[...], x_ref[...], precision=HIGH, preferred_element_type=jnp.float32)
    gram_ref[...] = fold(inner(y))
    blk = o_ref.shape[1]
    for i in range(all_ref.shape[0]):
        all_ref[i] = y[:, i * blk : (i + 1) * blk]
    o_ref[...] = all_ref[own_ref[0]]


def normal(own, inverse, slices):
    width, blk = slices[0].shape
    blocks = NS
    vmem = pl.BlockSpec(memory_space=pltpu.VMEM)
    return pl.pallas_call(
        normal_kernel,
        out_shape=(
            jax.ShapeDtypeStruct((width, blk), jnp.float32),
            jax.ShapeDtypeStruct((width // 2 + 8, width), jnp.float32),
        ),
        in_specs=[pl.BlockSpec(memory_space=pltpu.SMEM)] + [vmem] * (1 + len(slices)),
        scratch_shapes=[
            pltpu.VMEM((width, blocks * blk), jnp.float32),
            pltpu.VMEM((blocks, width, blk), jnp.float32),
        ],
        compiler_params=GRANT,
        name="normal",
    )(own.reshape(1), inverse, *slices)


def ends_kernel(bounds_ref, centre_ref, half_ref):
    centre_ref[...] = jnp.full(centre_ref.shape, (bounds_ref[0] + bounds_ref[1]) / 2.0)
    half_ref[...] = jnp.full(half_ref.shape, (bounds_ref[1] - bounds_ref[0]) / 2.0)


def ends(bounds, width):
    row = jax.ShapeDtypeStruct((1, width), jnp.float32)
    return pl.pallas_call(
        ends_kernel,
        out_shape=(row, row),
        in_specs=[pl.BlockSpec(memory_space=pltpu.SMEM)],
        compiler_params=GRANT,
        name="ends",
    )(bounds)


def on_device(start_block, tiles, tile_rows, tile_cols, bounds):
    blk = tiles.shape[1]
    centre, half = ends(bounds, blk)
    width = start_block.shape[1]
    total_rows = blk * 2 ** len(AXES)
    own = 0
    for name in SPLIT:
        own = own * 2 + lax.axis_index(name)
    own_row = 2 * lax.axis_index("ylo") + lax.axis_index("core")
    tie = lax.optimization_barrier

    start_block, centre, half = tie((start_block, centre, half))
    slots = tile_rows.shape[0]
    notes = jnp.pad(jnp.stack([tile_rows, tile_cols]).astype(jnp.float32), ((0, 6), (0, blk - slots)))
    slices = start_block.T.reshape(NS, width // NS, blk)
    slices = jnp.concatenate([slices, jnp.broadcast_to(notes, (NS, *notes.shape))], axis=1)
    near = exchange(jnp.concatenate([slices, slices], axis=0), ("ylo",) + SPLIT)
    tile_sets, near = share_tiles(tiles, near)
    begun = [near, swap(near, "core")]
    got = lax.dynamic_index_in_dim(near.reshape(2, NS, *near.shape[1:]), lax.axis_index("ylo"), 0, keepdims=False)
    current = got[:, : width // NS].reshape(width, blk)
    all_rows, all_cols = (got[:, width // NS + i, :slots].astype(jnp.int32) for i in range(2))
    live = all_rows >= 0
    member = jnp.arange(NS, dtype=jnp.int32)[:, None]
    source = jnp.where(live, (4 - (all_cols ^ own_row)) % 4 * NS + member, 4 * NS).reshape(-1)
    column = (all_cols ^ lax.axis_index("core")) % 2 * 2 + all_cols // 2
    source_begun = jnp.where(live, column * NS + member, 4 * NS).reshape(-1)
    place = jnp.where(live, digits(all_rows, SCATTER) * NS + digits(all_rows, SPLIT), 0).reshape(-1)
    early = sum(t.shape[0] for t in tile_sets[:-1])

    part = width // NS

    def multiply(v, others, **riders):
        return exchange(product(own, place, source, [v, *others], tile_sets, part, **riders), SCATTER)

    def multiply_first(small):
        prods = product(own, place, source_begun, begun, tile_sets[:-1], part)
        prods, small = tie((prods, small))
        return small, exchange(product(own, place, source_begun, begun, tile_sets[-1:], part, early, prods), SCATTER)

    def add_up(got):
        return jnp.sum(got, axis=0)

    def add_three(x, others):
        return (x + others[0]) + (others[1] + others[2])

    (current, centre, half), got = multiply_first((current, centre, half))
    first = (add_up(got) - centre * current) / half
    second = 2.0 * (add_up(multiply(first, three(first, ROW))) - centre * first) / half - current
    third = 2.0 * (add_up(multiply(second, three(second, ROW))) - centre * second) / half - first

    current = third
    first = (add_up(multiply(current, three(current, ROW))) - centre * current) / half
    slices = three(current, SPLIT)
    others = three(first, ROW)
    got = add_up(multiply(first, others, cut=gram(own, [current, *slices])))
    second = 2.0 * (got[:width] - centre * first) / half - current
    second = jnp.concatenate([second, got[width:]], axis=0)
    got = multiply(second, three(second, ROW), add=True)
    third = 2.0 * (add_up(got[:, :width]) - centre * second[:width]) / half - first
    inverse = factor(got)

    block, local = normal(own, inverse, [third, *three(third, SPLIT)])
    local = add_three(local, three(local, ROW))
    folded = exchange(jnp.broadcast_to(local, (NM, *local.shape)), SCATTER)
    return finish(folded, block, math.sqrt(total_rows))


def solution(mesh):
    fine = Mesh(mesh.devices.reshape((2,) * len(AXES)), AXES)
    return jax.shard_map(
        on_device,
        mesh=fine,
        in_specs=(P(AXES, None), P(AXES, None, None), P(AXES), P(AXES), P()),
        out_specs=P(AXES, None),
        check_vma=False,
    )
```

```python
import functools
import math

import jax
import jax.numpy as jnp
from jax import lax
from jax.experimental import pallas as pl
from jax.experimental.pallas import tpu as pltpu
from jax.sharding import Mesh
from jax.sharding import PartitionSpec as P

ITERS = 2
HIGH = lax.Precision.HIGHEST
AXES = ("ylo", "core", "zhi", "zlo", "xhi", "xlo", "yhi")
ROW = ("ylo", "core")
COL = ("zhi", "zlo", "xhi", "xlo", "yhi")
SPLIT = ("xhi", "yhi")
SCATTER = ("xlo", "zlo", "zhi")
NS = 2 ** len(SPLIT)
NM = 2 ** len(SCATTER)
GRANT = pltpu.CompilerParams(vmem_limit_bytes=16 * 2**20)


def cost(micros):
    return pl.CostEstimate(flops=0, bytes_accessed=int(micros * 1.2e6), transcendentals=0)


def digits(index, names):
    out = 0
    for name in names:
        shift = len(COL) - 1 - COL.index(name)
        out = out * 2 + ((index >> shift) & 1)
    return out


def swap(x, name):
    return lax.ppermute(x, name, [(0, 1), (1, 0)])


def three(x, names):
    return [lax.ppermute(x, names, [(i, i ^ 3) for i in range(4)]), swap(x, names[0]), swap(x, names[1])]


def exchange(x, names):
    if not names:
        return x
    return lax.all_to_all(x, names, 0, 0, tiled=True)


def turn(tile):
    size = tile.shape[0]
    row = lax.broadcasted_iota(jnp.int32, (size, size), 0)
    column = lax.broadcasted_iota(jnp.int32, (size, size), 1)
    identity = jnp.where(row == column, 1.0, 0.0).astype(tile.dtype)
    return lax.dot_general(identity, tile, (((1,), (1,)), ((), ())), preferred_element_type=jnp.float32)


def widen_kernel(tiles_ref, a_ref, b_ref):
    slots, blk, _ = tiles_ref.shape
    half = slots // 2
    for i in range(half):
        a_ref[i * blk : (i + 1) * blk, :] = turn(tiles_ref[i])
        b_ref[i * blk : (i + 1) * blk, :] = turn(tiles_ref[half + i])


def widen(tiles):
    slots, blk, _ = tiles.shape
    wide = jax.ShapeDtypeStruct((slots // 2 * blk, blk), jnp.float32)
    return pl.pallas_call(
        widen_kernel,
        out_shape=(wide, wide),
        compiler_params=GRANT,
        cost_estimate=cost(1.3), name="widen",
    )(tiles)


def turn_kernel(tiles_ref, o_ref):
    for i in range(tiles_ref.shape[0]):
        o_ref[i] = turn(tiles_ref[i]).astype(o_ref.dtype)


def turn_all(tiles):
    return pl.pallas_call(
        turn_kernel,
        out_shape=jax.ShapeDtypeStruct(tiles.shape, tiles.dtype),
        compiler_params=GRANT,
        cost_estimate=cost(0.5), name="turn",
    )(tiles)


def pack_kernel(*refs):
    o_ref = refs[-1]
    _, step, blk, _ = o_ref.shape
    for i, r in enumerate(refs[:-1]):
        for k in range(step):
            o_ref[i, k] = r[k * blk : (k + 1) * blk, :].astype(o_ref.dtype)


def pack(parts, slots):
    blk = parts[0].shape[1]
    step = 4
    spec = pl.BlockSpec((step * blk, blk), lambda i: (i, 0))
    return pl.pallas_call(
        pack_kernel,
        grid=(slots // step,),
        out_shape=jax.ShapeDtypeStruct((len(parts), slots, blk, blk), jnp.bfloat16),
        in_specs=[spec] * len(parts),
        out_specs=pl.BlockSpec((len(parts), step, blk, blk), lambda i: (0, i, 0, 0)),
        compiler_params=GRANT,
        cost_estimate=cost(1.3), name="pack",
    )(*parts).reshape(-1, blk, blk)


def share_tiles(tiles, small):
    half = tiles.shape[0] // 2
    a, b = widen(tiles)
    a_y, b_x = swap(a, "yhi"), swap(b, "xhi")
    a_x, b_y = swap(a, "xhi"), swap(b, "yhi")
    a_xy, b_xy = swap(a_y, "xhi"), swap(b_x, "yhi")
    _, tiles = lax.optimization_barrier((a_x, tiles))
    return (turn_all(tiles), pack([a_y, b_y, a_x, b_x], half), pack([a_xy, b_xy], half)), small


def product_kernel(count, begun, rider, start, own_ref, place_ref, source_ref, *refs):
    v_refs, refs, o_ref, parts = refs[:count], refs[count:-2], refs[-2], refs[-1]
    tile_refs = refs[: len(refs) - begun - (rider == "cut")]
    blocks, rows, blk = parts.shape
    width = rows // 3
    at = 0
    for v_ref in v_refs:
        for i in range((blocks - 1) // count):
            v = v_ref[i, :width] if len(v_ref.shape) == 3 else v_ref[i * width : (i + 1) * width]
            high = v.astype(jnp.bfloat16)
            rest = v - high.astype(jnp.float32)
            middle = rest.astype(jnp.bfloat16)
            parts[at, 0:width, :] = high
            parts[at, width : 2 * width, :] = middle
            parts[at, 2 * width :, :] = (rest - middle.astype(jnp.float32)).astype(jnp.bfloat16)
            at += 1
    parts[at] = jnp.zeros(parts.shape[1:], jnp.bfloat16)
    o_ref[...] = refs[-1][...] if begun else jnp.zeros_like(o_ref)
    slots = place_ref.shape[0] // NS
    at = start
    for tiles_ref in tile_refs:
        for t in range(tiles_ref.shape[0]):
            slot = (own_ref[0] ^ (at // slots)) * slots + at % slots
            at += 1
            p = lax.dot_general(
                parts[source_ref[slot]],
                tiles_ref[t],
                (((1,), (0,)), ((), ())),
                preferred_element_type=jnp.float32,
            )
            place = place_ref[slot]
            to = pl.ds(pl.multiple_of(place % NS * width, width), width)
            o_ref[place // NS, to, :] += p[0:width] + p[width : 2 * width] + p[2 * width :]
    members, total, _ = o_ref.shape
    extra = total - NS * width
    for m in range(members):
        if rider == "cut":
            o_ref[m, NS * width :, :] = refs[-1][m * extra : (m + 1) * extra, :]
        if rider == "sum":
            x = [r[NS * width :, :] for r in v_refs]
            o_ref[m, NS * width :, :] = (x[0] + x[1]) + (x[2] + x[3])


def product(own, place, source, vs, tiles, width, start=0, begun=None, cut=None, add=False):
    blk = tiles[0].shape[-1]
    blocks = 4 * NS
    rider = "cut" if cut is not None else "sum" if add else None
    extra = cut.shape[0] // NM if cut is not None else vs[0].shape[0] - NS * width if add else 0
    smem = pl.BlockSpec(memory_space=pltpu.SMEM)
    vmem = pl.BlockSpec(memory_space=pltpu.VMEM)
    last = [x for x in (begun, cut) if x is not None]
    return pl.pallas_call(
        functools.partial(product_kernel, len(vs), begun is not None, rider, start),
        out_shape=jax.ShapeDtypeStruct((NM, NS * width + extra, blk), jnp.float32),
        in_specs=[smem] * 3 + [vmem] * (len(vs) + len(tiles) + len(last)),
        out_specs=vmem,
        scratch_shapes=[pltpu.VMEM((blocks + 1, 3 * width, blk), jnp.bfloat16)],
        compiler_params=GRANT,
        cost_estimate=cost(1.4), name="product",
    )(own.reshape(1), place, source, *vs, *tiles, *last)


def factor_solve(gram, right):
    size = gram.shape[0]
    count = size // 8

    def spread(x):
        return jnp.broadcast_to(x, (8, size))

    left = [gram[8 * r : 8 * r + 8, :] for r in range(count)]
    right = list(right)
    out = []
    for p in range(count):
        steps, rows = [], []
        for r in range(p, count):
            columns = [spread(left[r][:, 8 * p + m : 8 * p + m + 1]) for m in range(8)]
            for j in range(8):
                if r == p:
                    scale = lax.rsqrt(spread(columns[j][j : j + 1, :]))
                    others = [spread(columns[m][j : j + 1, :]) * scale for m in range(j + 1, 8)]
                    steps.append((scale, others, spread(left[r][j : j + 1, :]) * scale, spread(right[r][j : j + 1, :]) * scale))
                    rows.append(steps[j][3][0:1])
                scale, others, up, row = steps[j]
                entry = columns[j] * scale
                for m in range(j + 1, 8):
                    columns[m] = columns[m] - entry * others[m - j - 1]
                left[r] = left[r] - entry * up
                right[r] = right[r] - entry * row
        out.append(jnp.concatenate(rows, axis=0))
    return out


def factor_kernel(got_ref, o_ref):
    size = o_ref.shape[0]
    extra = size // got_ref.shape[0]
    gram = jnp.concatenate([got_ref[m, got_ref.shape[1] - extra :, :] for m in range(got_ref.shape[0])], axis=0)
    lane = lax.broadcasted_iota(jnp.int32, (8, size), 1)
    sub = lax.broadcasted_iota(jnp.int32, (8, size), 0)
    identity = [jnp.where(lane == sub + 8 * r, 1.0, 0.0) for r in range(size // 8)]
    for i, rows in enumerate(factor_solve(gram, identity)):
        o_ref[8 * i : 8 * i + 8, :] = rows


def factor(got):
    size = got.shape[2]
    return pl.pallas_call(
        factor_kernel,
        out_shape=jax.ShapeDtypeStruct((size, size), jnp.float32),
        compiler_params=GRANT,
        cost_estimate=cost(3.9), name="factor",
    )(got)


def fold(gram):
    half = gram.shape[0] // 2
    row = lax.broadcasted_iota(jnp.int32, (half, 2 * half), 0)
    column = lax.broadcasted_iota(jnp.int32, (half, 2 * half), 1) - half
    top, low = gram[:half], gram[half:]
    body = jnp.where((column < 0) | (row < column), low, pltpu.roll(top, half, 1))
    diagonal = jnp.sum(jnp.where(row == column, low, 0.0), axis=0, keepdims=True)
    return jnp.concatenate([body, jnp.broadcast_to(diagonal, (8, 2 * half))], axis=0)


def unfold(folded):
    half = folded.shape[1] // 2
    row = lax.broadcasted_iota(jnp.int32, (half, 2 * half), 0)
    column = lax.broadcasted_iota(jnp.int32, (half, 2 * half), 1)
    body, diagonal = folded[:half], folded[half : half + 1]
    turned = jnp.concatenate([body, jnp.zeros_like(body)], axis=0).T
    beside, below = turned[:half], turned[half:]
    first = jnp.where(row >= column, pltpu.roll(body, half, 1), below)
    top = jnp.where(column < half, first, pltpu.roll(beside, half, 1))
    column = column - half
    last = jnp.where(row == column, diagonal, pltpu.roll(below, half, 1))
    low = jnp.where((column < 0) | (row < column), body, last)
    return jnp.concatenate([top, low], axis=0)


def finish_kernel(scale, folded_ref, x_ref, o_ref):
    folded = folded_ref[0]
    for i in range(1, folded_ref.shape[0]):
        folded = folded + folded_ref[i]
    x = [x_ref[8 * r : 8 * r + 8, :] for r in range(x_ref.shape[0] // 8)]
    x = factor_solve(unfold(folded), x)
    o_ref[...] = jnp.concatenate(x, axis=0).T * scale


def finish(folded, x, scale):
    return pl.pallas_call(
        functools.partial(finish_kernel, scale),
        out_shape=jax.ShapeDtypeStruct(x.shape[::-1], jnp.float32),
        compiler_params=GRANT,
        cost_estimate=cost(4.7), name="finish",
    )(folded, x)


def join(own, refs, x_ref):
    blk = refs[0].shape[1]
    width = x_ref.shape[0] // NS
    for i, r in enumerate(refs):
        rows = pl.ds(pl.multiple_of((own ^ (4 - i) % 4) * width, width), width)
        for b in range(NS):
            x_ref[rows, b * blk : (b + 1) * blk] = r[b * width : (b + 1) * width]


def inner(x):
    return lax.dot_general(x, x, (((1,), (1,)), ((), ())), precision=HIGH, preferred_element_type=jnp.float32)


def gram_kernel(own_ref, *refs):
    o_ref, x_ref = refs[-2:]
    join(own_ref[0], refs[:-2], x_ref)
    o_ref[...] = inner(x_ref[...])


def gram(own, slices):
    width, blk = slices[0].shape
    blocks = NS
    vmem = pl.BlockSpec(memory_space=pltpu.VMEM)
    return pl.pallas_call(
        gram_kernel,
        out_shape=jax.ShapeDtypeStruct((width, width), jnp.float32),
        in_specs=[pl.BlockSpec(memory_space=pltpu.SMEM)] + [vmem] * len(slices),
        scratch_shapes=[pltpu.VMEM((width, blocks * blk), jnp.float32)],
        compiler_params=GRANT,
        cost_estimate=cost(0.4), name="gram",
    )(own.reshape(1), *slices)


def normal_kernel(own_ref, inverse_ref, *refs):
    o_ref, gram_ref, x_ref, all_ref = refs[-4:]
    join(own_ref[0], refs[:-4], x_ref)
    y = jnp.dot(inverse_ref[...], x_ref[...], precision=HIGH, preferred_element_type=jnp.float32)
    gram_ref[...] = fold(inner(y))
    blk = o_ref.shape[1]
    for i in range(all_ref.shape[0]):
        all_ref[i] = y[:, i * blk : (i + 1) * blk]
    o_ref[...] = all_ref[own_ref[0]]


def normal(own, inverse, slices):
    width, blk = slices[0].shape
    blocks = NS
    vmem = pl.BlockSpec(memory_space=pltpu.VMEM)
    return pl.pallas_call(
        normal_kernel,
        out_shape=(
            jax.ShapeDtypeStruct((width, blk), jnp.float32),
            jax.ShapeDtypeStruct((width // 2 + 8, width), jnp.float32),
        ),
        in_specs=[pl.BlockSpec(memory_space=pltpu.SMEM)] + [vmem] * (1 + len(slices)),
        scratch_shapes=[
            pltpu.VMEM((width, blocks * blk), jnp.float32),
            pltpu.VMEM((blocks, width, blk), jnp.float32),
        ],
        compiler_params=GRANT,
        cost_estimate=cost(0.9), name="normal",
    )(own.reshape(1), inverse, *slices)


def ends_kernel(bounds_ref, centre_ref, half_ref):
    centre_ref[...] = jnp.full(centre_ref.shape, (bounds_ref[0] + bounds_ref[1]) / 2.0)
    half_ref[...] = jnp.full(half_ref.shape, (bounds_ref[1] - bounds_ref[0]) / 2.0)


def ends(bounds, width):
    row = jax.ShapeDtypeStruct((1, width), jnp.float32)
    return pl.pallas_call(
        ends_kernel,
        out_shape=(row, row),
        in_specs=[pl.BlockSpec(memory_space=pltpu.SMEM)],
        compiler_params=GRANT,
        cost_estimate=cost(0.5), name="ends",
    )(bounds)


def on_device(start_block, tiles, tile_rows, tile_cols, bounds):
    blk = tiles.shape[1]
    centre, half = ends(bounds, blk)
    width = start_block.shape[1]
    total_rows = blk * 2 ** len(AXES)
    own = 0
    for name in SPLIT:
        own = own * 2 + lax.axis_index(name)
    own_row = 2 * lax.axis_index("ylo") + lax.axis_index("core")
    tie = lax.optimization_barrier

    start_block, centre, half = tie((start_block, centre, half))
    slots = tile_rows.shape[0]
    notes = jnp.pad(jnp.stack([tile_rows, tile_cols]).astype(jnp.float32), ((0, 6), (0, blk - slots)))
    slices = start_block.T.reshape(NS, width // NS, blk)
    slices = jnp.concatenate([slices, jnp.broadcast_to(notes, (NS, *notes.shape))], axis=1)
    near = exchange(jnp.concatenate([slices, slices], axis=0), ("ylo",) + SPLIT)
    tile_sets, near = share_tiles(tiles, near)
    begun = [near, swap(near, "core")]
    got = lax.dynamic_index_in_dim(near.reshape(2, NS, *near.shape[1:]), lax.axis_index("ylo"), 0, keepdims=False)
    current = got[:, : width // NS].reshape(width, blk)
    all_rows, all_cols = (got[:, width // NS + i, :slots].astype(jnp.int32) for i in range(2))
    live = all_rows >= 0
    member = jnp.arange(NS, dtype=jnp.int32)[:, None]
    source = jnp.where(live, (4 - (all_cols ^ own_row)) % 4 * NS + member, 4 * NS).reshape(-1)
    column = (all_cols ^ lax.axis_index("core")) % 2 * 2 + all_cols // 2
    source_begun = jnp.where(live, column * NS + member, 4 * NS).reshape(-1)
    place = jnp.where(live, digits(all_rows, SCATTER) * NS + digits(all_rows, SPLIT), 0).reshape(-1)
    early = sum(t.shape[0] for t in tile_sets[:-1])

    part = width // NS

    def multiply(v, others, **riders):
        return exchange(product(own, place, source, [v, *others], tile_sets, part, **riders), SCATTER)

    def multiply_first(small):
        prods = product(own, place, source_begun, begun, tile_sets[:-1], part)
        prods, small = tie((prods, small))
        return small, exchange(product(own, place, source_begun, begun, tile_sets[-1:], part, early, prods), SCATTER)

    def add_up(got):
        return jnp.sum(got, axis=0)

    def add_three(x, others):
        return (x + others[0]) + (others[1] + others[2])

    (current, centre, half), got = multiply_first((current, centre, half))
    first = (add_up(got) - centre * current) / half
    second = 2.0 * (add_up(multiply(first, three(first, ROW))) - centre * first) / half - current
    third = 2.0 * (add_up(multiply(second, three(second, ROW))) - centre * second) / half - first

    current = third
    first = (add_up(multiply(current, three(current, ROW))) - centre * current) / half
    slices = three(current, SPLIT)
    others = three(first, ROW)
    got = add_up(multiply(first, others, cut=gram(own, [current, *slices])))
    second = 2.0 * (got[:width] - centre * first) / half - current
    second = jnp.concatenate([second, got[width:]], axis=0)
    got = multiply(second, three(second, ROW), add=True)
    third = 2.0 * (add_up(got[:, :width]) - centre * second[:width]) / half - first
    inverse = factor(got)

    block, local = normal(own, inverse, [third, *three(third, SPLIT)])
    local = add_three(local, three(local, ROW))
    folded = exchange(jnp.broadcast_to(local, (NM, *local.shape)), SCATTER)
    return finish(folded, block, math.sqrt(total_rows))


def solution(mesh):
    fine = Mesh(mesh.devices.reshape((2,) * len(AXES)), AXES)
    return jax.shard_map(
        on_device,
        mesh=fine,
        in_specs=(P(AXES, None), P(AXES, None, None), P(AXES), P(AXES), P()),
        out_specs=P(AXES, None),
        check_vma=False,
    )
```
